256 devices in a mesh: section: 2 (over y_hi), freq: 64 (over y_lo, x, z), pos: 2 (over core).
Axes of the slice: x: 4, y: 4 (y_hi: 2, y_lo: 2; y = y_hi * 2 + y_lo), z: 8, core: 2. Of those that a mesh axis runs over, the one named last changes fastest.
Arguments:
- raw_capture: bfloat16 [4, 128, 128, 4096], P('pos', ('section', 'freq')), may hold values from -6 to 6
- band_bins: int32 [1024], replicated, may hold values from 64 to 1023
- probe_index: int32 [4], P('pos'), may hold values from 0 to 63
Outputs:
- panel_image: float32 [4, 512], P(None, ('section', 'freq'))
The draws below stay inside these ranges and needn't reach their ends.
All inputs are finite; a program needn't handle non-finite values.
Results may differ from the reference program's by a relative error of at most 0.0058.
Values may be sent and summed in bfloat16 or wider, within the bound.
A program may use at most 64 MiB of HBM per device.

```python
import math
import jax
import jax.numpy as jnp
from jax import lax

NE = 128
NT = 4096
NF = 1024
IX = 512
IZ = 4
POS = 4


def with_ends(array, own_key, low, high):
    extent = array.shape
    spot = [jax.random.randint(jax.random.fold_in(own_key, axis), (), 0, extent[axis]) for axis in range(len(extent))]
    array = array.at[tuple(spot)].set(low)
    longest = extent.index(max(extent))
    spot[longest] = (spot[longest] + 1) % extent[longest]
    return array.at[tuple(spot)].set(high)


def shard_levels(own_key, shape, cuts, smallest, largest):
    loudness = 1.0
    for dim, shards_of in cuts:
        heights = jax.random.uniform(jax.random.fold_in(jax.random.fold_in(own_key, 6), dim), (shards_of,), jnp.float32, smallest / len(cuts), largest / len(cuts))
        loudness = loudness * jnp.repeat(jnp.exp(heights), shape[dim] // shards_of).reshape((-1,) + (1,) * (len(shape) - 1 - dim))
    return loudness


def normal_values(own_key, extent, deviation, limit, pieces=(), kind=jnp.bfloat16):
    drawn = jax.random.normal(own_key, extent, jnp.float32) * deviation
    if len(pieces) > 0:
        drawn = shard_levels(own_key, extent, pieces, -0.22, 0.18) * drawn
    return jnp.clip(drawn, min=-limit, max=limit).astype(kind)


def setup_inputs(seed: int = 0) -> dict:
    keys = jax.random.split(jax.random.key(seed), 4)
    raw_capture = normal_values(keys[0], (POS, NE, NE, NT), 1.0, 6.0, ((0, 2), (1, 128)))
    band_bins = with_ends(jax.random.randint(keys[1], (NF,), NT // 64, NT // 4), jax.random.fold_in(keys[1], 1), NT // 64, (NT // 4) - 1).astype(jnp.int32)
    probe_index = with_ends(jax.random.randint(keys[2], (POS,), 0, 64), jax.random.fold_in(keys[2], 1), 0, 63).astype(jnp.int32)
    return {"raw_capture": raw_capture, "band_bins": band_bins, "probe_index": probe_index}


wave_speed = 0.5
pixel_pitch = 0.25
depth_start = 20.0
probe_anchor = 32.0

def time_table(band_bins, samples):
    sample_ids = jnp.arange(samples, dtype=jnp.int32)
    phase_turns = sample_ids[:, None] * band_bins[None, :] % samples
    phase_value = phase_turns.astype(jnp.float32) * (2.0 * math.pi / samples)
    return jnp.concatenate([jnp.cos(phase_value), -jnp.sin(phase_value)], axis=1).astype(jnp.bfloat16)

def element_table(elems):
    element_pos = jnp.arange(elems, dtype=jnp.float32) - (elems - 1) / 2.0
    wavenumber = (jnp.arange(elems, dtype=jnp.float32) - elems // 2) * (2.0 * math.pi / elems)
    phase_angle = element_pos[:, None] * wavenumber[None, :]
    cosine = jnp.cos(phase_angle)
    sine_part = jnp.sin(phase_angle)
    upper_rows = jnp.concatenate([cosine, -sine_part], axis=1)
    lower_rows = jnp.concatenate([sine_part, cosine], axis=1)
    return jnp.concatenate([upper_rows, lower_rows], axis=0).astype(jnp.bfloat16)

def focus_bin(spectrum, bin_value, index_value, tx_coord, samples):
    elems = spectrum.shape[1] // 2
    across = jnp.tile(jnp.arange(IX, dtype=jnp.float32) * pixel_pitch, IZ)
    depth_rows = jnp.repeat(depth_start + jnp.arange(IZ, dtype=jnp.float32) * pixel_pitch, IX)
    centre = probe_anchor + index_value.astype(jnp.float32)
    wave_number = bin_value.astype(jnp.float32) * (2.0 * math.pi / samples) / wave_speed
    lateral = across - centre
    offset = lateral[None, :] - tx_coord[:, None]
    distance = jnp.sqrt(offset * offset + depth_rows[None, :] * depth_rows[None, :])
    send_phase = wave_number * distance
    wavenumber = (jnp.arange(elems, dtype=jnp.float32) - elems // 2) * (2.0 * math.pi / elems)
    vertical = jnp.sqrt(jnp.maximum(wave_number * wave_number - wavenumber * wavenumber, 0.0))
    weight = vertical / wave_number
    recv_phase = wavenumber[:, None] * lateral[None, :] + vertical[:, None] * depth_rows[None, :]
    recv_real = weight[:, None] * jnp.cos(recv_phase)
    recv_imag = weight[:, None] * jnp.sin(recv_phase)
    recv_table = jnp.concatenate([jnp.concatenate([recv_real, recv_imag], axis=1), jnp.concatenate([-recv_imag, recv_real], axis=1)], axis=0).astype(jnp.bfloat16)
    field_sum = jnp.dot(spectrum, recv_table, preferred_element_type=jnp.float32)
    pixels = across.shape[0]
    return lax.optimization_barrier(jnp.sum(jnp.cos(send_phase) * field_sum[:, :pixels] - jnp.sin(send_phase) * field_sum[:, pixels:], axis=0))

def reference(raw_capture, band_bins, probe_index):
    dft_table = time_table(band_bins, NT)
    element_dft = element_table(NE)

    def transform(position):
        spectrum = jnp.dot(position.reshape(NE * NE, NT), dft_table, preferred_element_type=jnp.float32).astype(jnp.bfloat16)
        stacked = spectrum.reshape(NE, NE, 2, NF).transpose(3, 0, 2, 1).reshape(NF * NE, 2 * NE)
        wave_rows = jnp.dot(stacked, element_dft, preferred_element_type=jnp.float32)
        return wave_rows.astype(jnp.bfloat16).reshape(NF, NE, 2 * NE)
    wavefield = lax.map(transform, raw_capture)
    tx_coord = jnp.arange(NE, dtype=jnp.float32) - (NE - 1) / 2.0

    def per_bin(image_sum, inputs):
        bin_value, slab_data = inputs
        for member in range(POS):
            image_sum = image_sum + focus_bin(slab_data[member], bin_value, probe_index[member], tx_coord, NT)
        return (image_sum, None)
    image_sum, _ = lax.scan(per_bin, jnp.zeros((IZ * IX,), jnp.float32), (band_bins, wavefield.transpose(1, 0, 2, 3)))
    image_scale = 1.0 / math.sqrt(float(NT * NE ** 3 * NF * POS))
    return (image_sum * image_scale).reshape(IZ, IX)
```

```python
import functools
import math

import jax
import jax.numpy as jnp
import ml_dtypes
import numpy as np
from jax import lax
from jax.experimental import pallas as pl
from jax.experimental.pallas import tpu as pltpu
from jax.sharding import PartitionSpec as P

NE = 128
NT = 4096
NF = 1024
IX = 512
IZ = 4
POS_HERE = 2
RADIX = 16
QUARTER = NT // 4
CENTRES = 64

wave_speed = 0.5
pixel_pitch = 0.25
depth_start = 20.0
probe_anchor = 32.0

EVEN = ((0, 8, 4, -4), (2, -2, 6, -6))
ODD = ((1, 5, -3, -7), (3, 7, -1, -5))


def group_of(offset):
    if offset in (0, 8):
        return 7, 8 * offset
    return abs(offset) - 1, 0 if offset > 0 else CENTRES


def time_tables():
    samples = np.arange(QUARTER)
    centres = RADIX * (np.arange(CENTRES) + 1)

    def parts(offsets):
        bins = np.concatenate([centres + offset for offset in offsets])
        angle = 2.0 * np.pi * (bins[:, None] * samples[None, :] % NT) / NT
        return np.cos(angle), -np.sin(angle)

    even = np.stack([np.concatenate(parts(offsets), axis=0) for offsets in EVEN])
    re1, im1 = parts(ODD[0])
    re3, im3 = parts(ODD[1])
    odd = np.concatenate(
        [np.concatenate([re1, im1], axis=1), np.concatenate([im3, re3], axis=1)], axis=0
    )
    return even.astype(ml_dtypes.bfloat16), odd.astype(ml_dtypes.bfloat16)


def element_table():
    pos = np.arange(NE) - (NE - 1) / 2.0
    angle = pos[:, None] * (np.arange(NE) - NE // 2)[None, :] * (2.0 * np.pi / NE)
    c, s = np.cos(angle), np.sin(angle)
    table = np.concatenate([np.concatenate([c, -s], axis=1), np.concatenate([s, c], axis=1)], axis=0)
    return table.astype(ml_dtypes.bfloat16)


def column_table():
    order = np.arange(NE) - NE // 2
    angle = 2.0 * np.pi * (order[:, None] * np.arange(IX)[None, :] % IX) / IX
    cosine, sine = np.cos(angle), np.sin(angle)
    tiles = []
    for start in range(0, IX, 128):
        c, s = cosine[:, start : start + 128], sine[:, start : start + 128]
        tiles.append(
            np.concatenate([np.concatenate([c, s], axis=1), np.concatenate([-s, c], axis=1)], axis=0)
        )
    return np.stack(tiles).astype(ml_dtypes.bfloat16)


def depth_table():
    centres = RADIX * (np.arange(CENTRES) + 1)
    wavenumber = (np.arange(NE) - NE // 2) * (2.0 * np.pi / NE)

    def parts(offset):
        k = (centres + offset)[:, None] * (2.0 * np.pi / NT) / wave_speed
        vertical = np.sqrt(np.maximum(k * k - wavenumber[None, :] ** 2, 0.0))
        weight = vertical / k
        first = weight * np.exp(1j * vertical * depth_start)
        step = np.exp(1j * vertical * pixel_pitch)
        return np.stack([first.real, first.imag, step.real, step.imag])

    groups = [np.concatenate([parts(offset), parts(-offset)], axis=1) for offset in range(1, 8)]
    groups.append(np.concatenate([parts(0), parts(8)], axis=1))
    return np.stack(groups, axis=1).astype(np.float32)


def turn_pair(turns):
    x = turns - jnp.floor(turns + 0.5)
    square = x * x
    sine = jnp.full_like(x, math.pi**13 / math.factorial(13))
    for power in (11, 9, 7, 5, 3, 1):
        sign = 1.0 if power % 4 == 1 else -1.0
        sine = sine * square + sign * math.pi**power / math.factorial(power)
    sine = sine * x
    cosine = jnp.full_like(x, math.pi**12 / math.factorial(12))
    for power in (10, 8, 6, 4, 2, 0):
        sign = 1.0 if power % 4 == 0 else -1.0
        cosine = cosine * square + sign * math.pi**power / math.factorial(power)
    return 1.0 - 2.0 * sine * sine, 2.0 * sine * cosine


def transposed_dot(a, b):
    return lax.dot_general(a, b, (((1,), (1,)), ((), ())), preferred_element_type=jnp.float32)


def focus_kernel(
    probe_ref, tx_ref, bins_ref, raw_ref, even_ref, odd_ref, element_ref, column_ref, depth_ref,
    out_ref, negative, spectra, rows, counts, near, far, image,
):
    bins = bins_ref[...]
    centre = (bins - 9) >> 4
    offset = bins - 16 * centre - 16
    is_centre = jnp.where(lax.broadcasted_iota(jnp.int32, (CENTRES, NF), 0) == centre, 1.0, 0.0)
    is_offset = jnp.where(lax.broadcasted_iota(jnp.int32, (16, NF), 0) - 7 == offset, 1.0, 0.0)
    counts[...] = transposed_dot(is_centre.astype(jnp.bfloat16), is_offset.astype(jnp.bfloat16))

    sub = lax.broadcasted_iota(jnp.int32, (8, 128), 0).astype(jnp.float32) + 1.0
    lane = lax.broadcasted_iota(jnp.int32, (8, 128), 1)
    for p in range(POS_HERE):
        shift = 4 * (probe_ref[p] + int(probe_anchor))
        middle = probe_anchor + probe_ref[p].astype(jnp.float32)
        for tile in range(IX // 128):
            column = ((lane + (128 * tile + shift)) & (IX - 1)).astype(jnp.float32)
            x = (pixel_pitch * column - middle) - tx_ref[0]
            for k in range(IZ):
                z = depth_start + pixel_pitch * k
                turns = jnp.sqrt(x * x + z * z) * (1.0 / (NT * wave_speed))
                c, s = turn_pair(turns * sub)
                near[tile, p * IZ + k, 0], near[tile, p * IZ + k, 1] = c, s
                c, s = turn_pair(turns * (sub * RADIX))
                far[tile, p * IZ + k, 0], far[tile, p * IZ + k, 1] = c, s

    negative[...] = -raw_ref[...]

    def quarters(signs):
        return jnp.concatenate(
            [
                (raw_ref if sign > 0 else negative)[:, q * QUARTER : (q + 1) * QUARTER]
                for q, sign in enumerate(signs)
            ],
            axis=1,
        )

    def keep(values, offsets, part):
        for index, offset in enumerate(offsets):
            group, row = group_of(offset)
            for p in range(POS_HERE):
                spectra[p, group, row : row + CENTRES, part * NE : (part + 1) * NE] = values[
                    index * CENTRES : (index + 1) * CENTRES, p * NE : (p + 1) * NE
                ]

    for index, signs in enumerate(((1, 1, 1, 1), (1, -1, 1, -1))):
        table = even_ref[index]
        out = transposed_dot(jnp.concatenate([table] * 4, axis=1), quarters(signs)).astype(jnp.bfloat16)
        keep(out[: 4 * CENTRES], EVEN[index], 0)
        keep(out[4 * CENTRES :], EVEN[index], 1)
    left, right = odd_ref[:, :QUARTER], odd_ref[:, QUARTER:]
    out = transposed_dot(
        jnp.concatenate([left, right, left, right], axis=1), quarters((1, 1, -1, -1))
    ).astype(jnp.bfloat16)
    keep(out[: 4 * CENTRES], ODD[0], 0)
    keep(out[4 * CENTRES :], ODD[1], 1)
    out = transposed_dot(
        jnp.concatenate([right, left, right, left], axis=1), quarters((1, -1, -1, 1))
    ).astype(jnp.bfloat16)
    keep(out[: 4 * CENTRES], ODD[0], 1)
    keep(out[4 * CENTRES :], ODD[1], 0)

    for group in range(8):
        scales = [
            counts[:, 7 + o : 8 + o] for o in ((group + 1, -group - 1) if group < 7 else (0, 8))
        ]
        for p in range(POS_HERE):
            field = jnp.dot(spectra[p, group], element_ref[...], preferred_element_type=jnp.float32)
            field = field.astype(jnp.bfloat16)
            for block in range(0, CENTRES, 16):
                parts = []
                for half in range(2):
                    at = slice(half * CENTRES + block, half * CENTRES + block + 16)
                    scale = scales[half][block : block + 16]
                    re = field[at, :NE].astype(jnp.float32) * scale
                    im = field[at, NE:].astype(jnp.float32) * scale
                    cosine, sine = depth_ref[0, group, at, :], depth_ref[1, group, at, :]
                    parts.append([re * cosine - im * sine, re * sine + im * cosine])
                for k in range(IZ):
                    if k > 0:
                        for half in range(2):
                            at = slice(half * CENTRES + block, half * CENTRES + block + 16)
                            cosine, sine = depth_ref[2, group, at, :], depth_ref[3, group, at, :]
                            re, im = parts[half]
                            parts[half] = [re * cosine - im * sine, re * sine + im * cosine]
                    (re, im), (re_low, im_low) = parts
                    if group < 7:
                        values = (re + re_low, im + im_low, re - re_low, im - im_low)
                    else:
                        values = (re, im, re_low, im_low)
                    re, im, re_low, im_low = [value.astype(jnp.bfloat16) for value in values]
                    top = slice(block, block + 16)
                    low = slice(CENTRES + block, CENTRES + block + 16)
                    rows[p * IZ + k, group, top, :NE] = re
                    rows[p * IZ + k, group, top, NE:] = im
                    rows[p * IZ + k, group, low, :NE] = re_low
                    rows[p * IZ + k, group, low, NE:] = im_low

    @pl.loop(0, IX // 128)
    def _(tile):
        weights = column_ref[tile]
        for pk in range(POS_HERE * IZ):
            total_re = jnp.zeros((CENTRES, 128), jnp.float32)
            total_im = jnp.zeros((CENTRES, 128), jnp.float32)
            for group in range(8):
                both = jnp.dot(rows[pk, group], weights, preferred_element_type=jnp.float32)
                c, s = near[tile, pk, 0, group : group + 1, :], near[tile, pk, 1, group : group + 1, :]
                low_re, low_im = both[CENTRES:, :128], both[CENTRES:, 128:]
                if group < 7:
                    total_re += c * both[:CENTRES, :128] - s * low_im
                    total_im += c * both[:CENTRES, 128:] + s * low_re
                else:
                    total_re += both[:CENTRES, :128] + (c * low_re - s * low_im)
                    total_im += both[:CENTRES, 128:] + (c * low_im + s * low_re)
            jump_cos = jnp.broadcast_to(far[tile, pk, 0, 7:8, :], (8, 128))
            jump_sin = jnp.broadcast_to(far[tile, pk, 1, 7:8, :], (8, 128))
            re, im = total_re[56:], total_im[56:]
            for g in range(6, -1, -1):
                re, im = (
                    re * jump_cos - im * jump_sin + total_re[8 * g : 8 * g + 8],
                    re * jump_sin + im * jump_cos + total_im[8 * g : 8 * g + 8],
                )
            value = re * far[tile, pk, 0] - im * far[tile, pk, 1]
            image[tile, pk : pk + 1, :] = jnp.sum(value, axis=0, keepdims=True)

    scale = 1.0 / math.sqrt(float(NT * NE**3 * NF * 4))
    both = jnp.concatenate([image[tile] for tile in range(IX // 128)], axis=1)
    shifts = [4 * (probe_ref[p] + int(probe_anchor)) for p in range(POS_HERE)]
    total = pltpu.roll(both, shifts[0], 1)[:IZ] + pltpu.roll(both, shifts[1], 1)[IZ:]
    for tile in range(IX // 128):
        out_ref[tile] = total[:, tile * 128 : (tile + 1) * 128] * scale


def focus(raw, band_bins, probe_index, tx_coord):
    even, odd = time_tables()
    vmem = pl.BlockSpec(memory_space=pltpu.VMEM)
    smem = pl.BlockSpec(memory_space=pltpu.SMEM)
    return pl.pallas_call(
        focus_kernel,
        out_shape=jax.ShapeDtypeStruct((IX // 128, IZ, 128), jnp.float32),
        in_specs=[smem, smem] + [vmem] * 7,
        out_specs=vmem,
        scratch_shapes=[
            pltpu.VMEM((POS_HERE * NE, NT), jnp.bfloat16),
            pltpu.VMEM((POS_HERE, 8, 128, 2 * NE), jnp.bfloat16),
            pltpu.VMEM((POS_HERE * IZ, 8, 128, 2 * NE), jnp.bfloat16),
            pltpu.VMEM((CENTRES, 16), jnp.float32),
            pltpu.VMEM((IX // 128, POS_HERE * IZ, 2, 8, 128), jnp.float32),
            pltpu.VMEM((IX // 128, POS_HERE * IZ, 2, 8, 128), jnp.float32),
            pltpu.VMEM((IX // 128, POS_HERE * IZ, 128), jnp.float32),
        ],
        compiler_params=pltpu.CompilerParams(vmem_limit_bytes=48 * 1024 * 1024),
        name="focus",
    )(
        probe_index,
        tx_coord,
        band_bins.reshape(1, NF),
        raw.reshape(POS_HERE * NE, NT),
        jnp.asarray(even),
        jnp.asarray(odd),
        jnp.asarray(element_table()),
        jnp.asarray(column_table()),
        jnp.asarray(depth_table()),
    )


MESH = pl.DeviceIdType.MESH


def combine_kernel(freqs, partial_ref, out_ref, inbox, middle, inbox2, send, recv, send2, recv2):
    section, freq, core = lax.axis_index("section"), lax.axis_index("freq"), lax.axis_index("pos")
    y = section * 2 + freq // 32
    x = freq // 8 % 4
    z = freq % 8
    plane = y * 4 + x
    pencil = z * 2 + core

    def plane_device(index):
        yy, xx = index // 4, index % 4
        return (yy // 2, yy % 2 * 32 + xx * 8 + z, core)

    def pencil_device(index):
        return (section, freq // 8 * 8 + index // 2, index % 2)

    barrier = pltpu.get_barrier_semaphore()
    for step in range(1, 16):
        pl.semaphore_signal(barrier, inc=1, device_id=plane_device((plane + step) % 16), device_id_type=MESH)
        pl.semaphore_signal(barrier, inc=1, device_id=pencil_device((pencil + step) % 16), device_id_type=MESH)
    pl.semaphore_wait(barrier, 30)

    copies = []
    for step in range(1, 16):
        to = (plane + step) % 16
        copy = pltpu.make_async_remote_copy(
            src_ref=partial_ref.at[to // 4],
            dst_ref=inbox.at[step - 1],
            send_sem=send.at[step - 1],
            recv_sem=recv.at[step - 1],
            device_id=plane_device(to),
            device_id_type=MESH,
        )
        copy.start()
        copies.append(copy)
    total = partial_ref[y]
    for step in range(1, 16):
        copies[step - 1].wait_recv()
        total = total + inbox[step - 1]
    middle[...] = total
    copies2 = []
    for step in range(1, 16):
        copy = pltpu.make_async_remote_copy(
            src_ref=middle,
            dst_ref=inbox2.at[step - 1],
            send_sem=send2.at[step - 1],
            recv_sem=recv2.at[step - 1],
            device_id=pencil_device((pencil + step) % 16),
            device_id_type=MESH,
        )
        copy.start()
        copies2.append(copy)
    for step in range(1, 16):
        copies2[step - 1].wait_recv()
        total = total + inbox2[step - 1]
    out_ref[...] = pltpu.roll(total, (128 - (x * 32 + z * 4)) % 128, 1)
    for copy in copies + copies2:
        copy.wait_send()


def combine(partial):
    vmem = pl.BlockSpec(memory_space=pltpu.VMEM)
    tile = (IZ, 128)
    return pl.pallas_call(
        functools.partial(combine_kernel, 64),
        out_shape=jax.ShapeDtypeStruct(tile, jnp.float32),
        in_specs=[vmem],
        out_specs=vmem,
        scratch_shapes=[
            pltpu.VMEM((15, *tile), jnp.float32),
            pltpu.VMEM(tile, jnp.float32),
            pltpu.VMEM((15, *tile), jnp.float32),
            pltpu.SemaphoreType.DMA((15,)),
            pltpu.SemaphoreType.DMA((15,)),
            pltpu.SemaphoreType.DMA((15,)),
            pltpu.SemaphoreType.DMA((15,)),
        ],
        compiler_params=pltpu.CompilerParams(collective_id=0, has_side_effects=True),
        name="combine",
    )(partial)


def per_device(raw_capture, band_bins, probe_index):
    transmitter = lax.axis_index(("section", "freq")).astype(jnp.float32)
    tx_coord = (transmitter - (NE - 1) / 2.0).reshape(1)
    partial = focus(raw_capture, band_bins, probe_index, tx_coord)
    return combine(partial)[:, :4]


def solution(mesh):
    in_specs = (P("pos", ("section", "freq"), None, None), P(), P("pos"))
    out_specs = P(None, ("section", "freq"))
    return jax.shard_map(
        per_device, mesh=mesh, in_specs=in_specs, out_specs=out_specs, check_vma=False
    )
```

```python
import math

import jax
import jax.numpy as jnp
import ml_dtypes
import numpy as np
from jax import lax
from jax.experimental import pallas as pl
from jax.experimental.pallas import tpu as pltpu
from jax.sharding import PartitionSpec as P

NE = 128
NT = 4096
NF = 1024
IX = 512
IZ = 4
POS_HERE = 2
QUARTER = NT // 4
LOWEST = 64
CENTRES = 48
SPACING = 20
FIRST = LOWEST + 9
GROUPS = 10
TILES = IX // 128
MESH = pl.DeviceIdType.MESH

wave_speed = 0.5
pixel_pitch = 0.25
depth_start = 20.0
probe_anchor = 32

EVEN = ((-9, -5, -1, 3, 7), (-7, -3, 1, 5, 9))
ODD = ((-8, -4, 0, 4, 8), (-6, -2, 2, 6, 10))


def group_of(offset):
    if offset in (0, 10):
        return GROUPS - 1, CENTRES * (offset // 10)
    return abs(offset) - 1, 0 if offset > 0 else CENTRES


def offsets_of(group):
    return (group + 1, -group - 1) if group < GROUPS - 1 else (0, 10)


def time_tables():
    samples = np.arange(QUARTER)
    centres = FIRST + SPACING * np.arange(CENTRES)

    def parts(offsets):
        bins = np.concatenate([centres + offset for offset in offsets])
        angle = 2.0 * np.pi * (bins[:, None] * samples[None, :] % NT) / NT
        return np.cos(angle), -np.sin(angle)

    even = np.stack([np.concatenate(parts(offsets), axis=0) for offsets in EVEN])
    re1, im1 = parts(ODD[0])
    re3, im3 = parts(ODD[1])
    odd = np.concatenate(
        [np.concatenate([re1, im1], axis=1), np.concatenate([im3, re3], axis=1)], axis=0
    )
    return even.astype(ml_dtypes.bfloat16), odd.astype(ml_dtypes.bfloat16)


def element_table():
    pos = np.arange(NE) - (NE - 1) / 2.0
    angle = pos[:, None] * (np.arange(NE) - NE // 2)[None, :] * (2.0 * np.pi / NE)
    c, s = np.cos(angle), np.sin(angle)
    table = np.concatenate([np.concatenate([c, -s], axis=1), np.concatenate([s, c], axis=1)], axis=0)
    return table.astype(ml_dtypes.bfloat16)


def column_table():
    order = np.arange(NE) - NE // 2
    angle = 2.0 * np.pi * (order[:, None] * np.arange(IX)[None, :] % IX) / IX
    cosine, sine = np.cos(angle), np.sin(angle)
    tiles = []
    for start in range(0, IX, 128):
        c, s = cosine[:, start : start + 128], sine[:, start : start + 128]
        tiles.append(
            np.concatenate([np.concatenate([c, s], axis=1), np.concatenate([-s, c], axis=1)], axis=0)
        )
    return np.stack(tiles).astype(ml_dtypes.bfloat16)


def depth_table():
    centres = FIRST + SPACING * np.arange(CENTRES)
    wavenumber = (np.arange(NE) - NE // 2) * (2.0 * np.pi / NE)

    def parts(offset):
        k = (centres + offset)[:, None] * (2.0 * np.pi / NT) / wave_speed
        vertical = np.sqrt(np.maximum(k * k - wavenumber[None, :] ** 2, 0.0))
        weight = vertical / k
        first = weight * np.exp(1j * vertical * depth_start)
        step = np.exp(1j * vertical * pixel_pitch)
        return np.stack([first.real, first.imag, step.real, step.imag])

    groups = [
        np.concatenate([parts(offset) for offset in offsets_of(group)], axis=1) for group in range(GROUPS)
    ]
    return np.stack(groups, axis=1).astype(np.float32)


def turn_pair(turns):
    x = turns - jnp.floor(turns + 0.5)
    square = x * x
    sine = jnp.full_like(x, math.pi**13 / math.factorial(13))
    for power in (11, 9, 7, 5, 3, 1):
        sign = 1.0 if power % 4 == 1 else -1.0
        sine = sine * square + sign * math.pi**power / math.factorial(power)
    sine = sine * x
    cosine = jnp.full_like(x, math.pi**12 / math.factorial(12))
    for power in (10, 8, 6, 4, 2, 0):
        sign = 1.0 if power % 4 == 0 else -1.0
        cosine = cosine * square + sign * math.pi**power / math.factorial(power)
    return 1.0 - 2.0 * sine * sine, 2.0 * sine * cosine


def transposed_dot(a, b):
    return lax.dot_general(a, b, (((1,), (1,)), ((), ())), preferred_element_type=jnp.float32)


def hops(count, delta):
    return min(delta, count - delta)


PLANE = sorted(
    [(dy, dx) for dy in range(4) for dx in range(4) if dy or dx],
    key=lambda d: -(hops(4, d[0]) + hops(4, d[1])),
)
PENCIL = sorted(
    [(dz, dc) for dz in range(8) for dc in range(2) if dz or dc],
    key=lambda d: -(2 * hops(8, d[0]) + d[1]),
)


def focus_kernel(
    probe_ref, bins_ref, raw_hbm, even_hbm, odd_hbm, element_hbm, column_hbm, depth_hbm,
    out_ref,
    raw_ref, even_ref, odd_ref, element_ref, column_ref, depth_ref, loaded,
    negative, spectra, rows, counts, near, far, image,
    partial, inbox, middle, inbox2, send, recv, send2, recv2,
):
    section, freq, core = lax.axis_index("section"), lax.axis_index("freq"), lax.axis_index("pos")
    y, x_chip, z_chip = section * 2 + (freq >> 5), (freq >> 3) & 3, freq & 7

    def plane_device(dy, dx):
        yy, xx = (y + dy) & 3, (x_chip + dx) & 3
        return (yy >> 1, (yy & 1) * 32 + xx * 8 + z_chip, core)

    def pencil_device(dz, dc):
        return (section, (freq & 56) + ((z_chip + dz) & 7), (core + dc) & 1)

    def load(index, source, target):
        return pltpu.make_async_copy(source, target, loaded.at[index])

    loads = [
        load(0, raw_hbm, raw_ref),
        load(1, even_hbm.at[0], even_ref.at[0]),
        load(2, even_hbm.at[1], even_ref.at[1]),
        load(3, odd_hbm, odd_ref),
        load(4, element_hbm, element_ref),
        load(5, depth_hbm, depth_ref),
        load(6, column_hbm, column_ref),
    ]
    for copy in loads[:2]:
        copy.start()

    barrier = pltpu.get_barrier_semaphore()
    for step in PLANE:
        pl.semaphore_signal(barrier, inc=1, device_id=plane_device(*step), device_id_type=MESH)
    for step in PENCIL:
        pl.semaphore_signal(barrier, inc=1, device_id=pencil_device(*step), device_id_type=MESH)

    bins = bins_ref[...] - LOWEST
    centre = (bins * 3277) >> 16
    offset = bins - SPACING * centre
    is_centre = jnp.where(lax.broadcasted_iota(jnp.int32, (CENTRES, NF), 0) == centre, 1.0, 0.0)
    is_offset = jnp.where(lax.broadcasted_iota(jnp.int32, (32, NF), 0) == offset, 1.0, 0.0)
    counts[...] = transposed_dot(is_centre.astype(jnp.bfloat16), is_offset.astype(jnp.bfloat16))

    tx_coord = (section * 64 + freq).astype(jnp.float32) - (NE - 1) / 2.0
    sub = lax.broadcasted_iota(jnp.int32, (16, 128), 0).astype(jnp.float32)
    near_powers = jnp.where(sub < 10.0, sub + 1.0, SPACING * 8.0)
    far_powers = FIRST + SPACING * sub[:8]
    lane = lax.broadcasted_iota(jnp.int32, (8, 128), 1)
    for p in range(POS_HERE):
        shift = 4 * (probe_ref[p] + probe_anchor)
        centre_here = (probe_ref[p] + probe_anchor).astype(jnp.float32)
        for tile in range(TILES):
            column = ((lane + (128 * tile + shift)) & (IX - 1)).astype(jnp.float32)
            x = (pixel_pitch * column - centre_here) - tx_coord
            for k in range(IZ):
                z = depth_start + pixel_pitch * k
                turns = jnp.sqrt(x * x + z * z) * (1.0 / (NT * wave_speed))
                c, s = turn_pair(jnp.concatenate([turns, turns], axis=0) * near_powers)
                near[tile, p * IZ + k, 0], near[tile, p * IZ + k, 1] = c, s
                c, s = turn_pair(turns * far_powers)
                far[tile, p * IZ + k, 0], far[tile, p * IZ + k, 1] = c, s

    def quarters(signs):
        return jnp.concatenate(
            [
                (raw_ref if sign > 0 else negative)[:, q * QUARTER : (q + 1) * QUARTER]
                for q, sign in enumerate(signs)
            ],
            axis=1,
        )

    def keep(values, offsets, part):
        for index, offset in enumerate(offsets):
            group, row = group_of(offset)
            for p in range(POS_HERE):
                spectra[p, group, row : row + CENTRES, part * NE : (part + 1) * NE] = values[
                    index * CENTRES : (index + 1) * CENTRES, p * NE : (p + 1) * NE
                ]

    def filtered(group, p):
        scales = [counts[:, 9 + o : 10 + o] for o in offsets_of(group)]
        field = jnp.dot(spectra[p, group], element_ref[...], preferred_element_type=jnp.float32)
        field = field.astype(jnp.bfloat16)
        for block in range(0, CENTRES, 16):
            parts = []
            for half in range(2):
                at = slice(half * CENTRES + block, half * CENTRES + block + 16)
                scale = scales[half][block : block + 16]
                re = field[at, :NE].astype(jnp.float32) * scale
                im = field[at, NE:].astype(jnp.float32) * scale
                cosine, sine = depth_ref[0, group, at, :], depth_ref[1, group, at, :]
                parts.append([re * cosine - im * sine, re * sine + im * cosine])
            for k in range(IZ):
                if k > 0:
                    for half in range(2):
                        at = slice(half * CENTRES + block, half * CENTRES + block + 16)
                        cosine, sine = depth_ref[2, group, at, :], depth_ref[3, group, at, :]
                        re, im = parts[half]
                        parts[half] = [re * cosine - im * sine, re * sine + im * cosine]
                (re, im), (re_low, im_low) = parts
                if group < GROUPS - 1:
                    values = (re + re_low, im + im_low, re - re_low, im - im_low)
                else:
                    values = (re, im, re_low, im_low)
                re, im, re_low, im_low = [value.astype(jnp.bfloat16) for value in values]
                top = slice(block, block + 16)
                low = slice(CENTRES + block, CENTRES + block + 16)
                rows[p * IZ + k, group, top, :NE] = re
                rows[p * IZ + k, group, top, NE:] = im
                rows[p * IZ + k, group, low, :NE] = re_low
                rows[p * IZ + k, group, low, NE:] = im_low

    half_rows = 5 * CENTRES
    loads[0].wait()
    loads[1].wait()
    for copy in loads[2:]:
        copy.start()
    negative[...] = -raw_ref[...]
    for index, signs in enumerate(((1, 1, 1, 1), (1, -1, 1, -1))):
        if index > 0:
            loads[2].wait()
        table = even_ref[index]
        out = transposed_dot(jnp.concatenate([table] * 4, axis=1), quarters(signs)).astype(jnp.bfloat16)
        keep(out[:half_rows], EVEN[index], 0)
        keep(out[half_rows:], EVEN[index], 1)
    for copy in loads[3:]:
        copy.wait()
    left, right = odd_ref[:, :QUARTER], odd_ref[:, QUARTER:]
    out = transposed_dot(
        jnp.concatenate([left, right, left, right], axis=1), quarters((1, 1, -1, -1))
    ).astype(jnp.bfloat16)
    keep(out[:half_rows], ODD[0], 0)
    keep(out[half_rows:], ODD[1], 1)
    out = transposed_dot(
        jnp.concatenate([right, left, right, left], axis=1), quarters((1, -1, -1, 1))
    ).astype(jnp.bfloat16)
    keep(out[:half_rows], ODD[0], 1)
    keep(out[half_rows:], ODD[1], 0)
    for p in range(POS_HERE):
        for group in range(GROUPS):
            filtered(group, p)

    @pl.loop(0, TILES)
    def _(tile):
        weights = column_ref[tile]
        for pk in range(POS_HERE * IZ):
            total_re = jnp.zeros((CENTRES, 128), jnp.float32)
            total_im = jnp.zeros((CENTRES, 128), jnp.float32)
            for group in range(GROUPS):
                both = jnp.dot(rows[pk, group], weights, preferred_element_type=jnp.float32)
                c, s = near[tile, pk, 0, group : group + 1, :], near[tile, pk, 1, group : group + 1, :]
                low_re, low_im = both[CENTRES:, :128], both[CENTRES:, 128:]
                if group < GROUPS - 1:
                    total_re += c * both[:CENTRES, :128] - s * low_im
                    total_im += c * both[:CENTRES, 128:] + s * low_re
                else:
                    total_re += both[:CENTRES, :128] + (c * low_re - s * low_im)
                    total_im += both[:CENTRES, 128:] + (c * low_im + s * low_re)
            jump_cos = jnp.broadcast_to(near[tile, pk, 0, 10:11, :], (8, 128))
            jump_sin = jnp.broadcast_to(near[tile, pk, 1, 10:11, :], (8, 128))
            re, im = total_re[CENTRES - 8 :], total_im[CENTRES - 8 :]
            for g in range(CENTRES // 8 - 2, -1, -1):
                re, im = (
                    re * jump_cos - im * jump_sin + total_re[8 * g : 8 * g + 8],
                    re * jump_sin + im * jump_cos + total_im[8 * g : 8 * g + 8],
                )
            value = re * far[tile, pk, 0] - im * far[tile, pk, 1]
            image[tile, pk : pk + 1, :] = jnp.sum(value, axis=0, keepdims=True)

    both = jnp.concatenate([image[tile] for tile in range(TILES)], axis=1)
    is_first = lax.broadcasted_iota(jnp.int32, (POS_HERE * IZ, IX), 0) < IZ
    turn = jnp.where(is_first, probe_ref[0] + probe_anchor, probe_ref[1] + probe_anchor)
    for bit in range(7):
        both = jnp.where(((turn >> bit) & 1) == 1, pltpu.roll(both, 4 << bit, 1), both)
    scale = 1.0 / math.sqrt(float(NT * NE**3 * NF * 4))
    for tile in range(TILES):
        columns = slice(tile * 128, (tile + 1) * 128)
        partial[tile] = (both[:IZ, columns] + both[IZ:, columns]) * scale

    pl.semaphore_wait(barrier, len(PLANE) + len(PENCIL))
    copies = []
    for index, step in enumerate(PLANE):
        copy = pltpu.make_async_remote_copy(
            src_ref=partial.at[(y + step[0]) & 3],
            dst_ref=inbox.at[index],
            send_sem=send.at[index],
            recv_sem=recv.at[index],
            device_id=plane_device(*step),
            device_id_type=MESH,
        )
        copy.start()
        copies.append(copy)
    total = partial[y]
    for index in reversed(range(len(PLANE))):
        copies[index].wait_recv()
        total = total + inbox[index]
    middle[...] = total
    copies2 = []
    for index, step in enumerate(PENCIL):
        copy = pltpu.make_async_remote_copy(
            src_ref=middle,
            dst_ref=inbox2.at[index],
            send_sem=send2.at[index],
            recv_sem=recv2.at[index],
            device_id=pencil_device(*step),
            device_id_type=MESH,
        )
        copy.start()
        copies2.append(copy)
    for index in reversed(range(len(PENCIL))):
        copies2[index].wait_recv()
        total = total + inbox2[index]
    out_ref[...] = pltpu.roll(total, (128 - (x_chip * 32 + z_chip * 4)) & 127, 1)
    for copy in copies + copies2:
        copy.wait_send()


def focus(raw, band_bins, probe_index):
    even, odd = time_tables()
    tables = [even, odd, element_table(), column_table(), depth_table()]
    vmem = pl.BlockSpec(memory_space=pltpu.VMEM)
    smem = pl.BlockSpec(memory_space=pltpu.SMEM)
    hbm = pl.BlockSpec(memory_space=pltpu.HBM)
    held = [pltpu.VMEM((POS_HERE * NE, NT), jnp.bfloat16)]
    held += [pltpu.VMEM(table.shape, table.dtype) for table in tables]
    tile = (IZ, 128)
    return pl.pallas_call(
        focus_kernel,
        out_shape=jax.ShapeDtypeStruct(tile, jnp.float32),
        in_specs=[smem, vmem] + [hbm] * 6,
        out_specs=vmem,
        scratch_shapes=[
            *held,
            pltpu.SemaphoreType.DMA((7,)),
            pltpu.VMEM((POS_HERE * NE, NT), jnp.bfloat16),
            pltpu.VMEM((POS_HERE, GROUPS, 2 * CENTRES, 2 * NE), jnp.bfloat16),
            pltpu.VMEM((POS_HERE * IZ, GROUPS, 2 * CENTRES, 2 * NE), jnp.bfloat16),
            pltpu.VMEM((CENTRES, 32), jnp.float32),
            pltpu.VMEM((TILES, POS_HERE * IZ, 2, 16, 128), jnp.float32),
            pltpu.VMEM((TILES, POS_HERE * IZ, 2, 8, 128), jnp.float32),
            pltpu.VMEM((TILES, POS_HERE * IZ, 128), jnp.float32),
            pltpu.VMEM((TILES, *tile), jnp.float32),
            pltpu.VMEM((15, *tile), jnp.float32),
            pltpu.VMEM(tile, jnp.float32),
            pltpu.VMEM((15, *tile), jnp.float32),
            pltpu.SemaphoreType.DMA((15,)),
            pltpu.SemaphoreType.DMA((15,)),
            pltpu.SemaphoreType.DMA((15,)),
            pltpu.SemaphoreType.DMA((15,)),
        ],
        compiler_params=pltpu.CompilerParams(
            collective_id=0, has_side_effects=True, vmem_limit_bytes=63 * 1024 * 1024
        ),
        name="focus",
    )(
        probe_index,
        band_bins.reshape(1, NF),
        raw.reshape(POS_HERE * NE, NT),
        *[jnp.asarray(table) for table in tables],
    )


def per_device(raw_capture, band_bins, probe_index):
    return focus(raw_capture, band_bins, probe_index)[:, :4]


def solution(mesh):
    in_specs = (P("pos", ("section", "freq"), None, None), P(), P("pos"))
    out_specs = P(None, ("section", "freq"))
    return jax.shard_map(
        per_device, mesh=mesh, in_specs=in_specs, out_specs=out_specs, check_vma=False
    )
```

```python
import math

import jax
import jax.numpy as jnp
import ml_dtypes
import numpy as np
from jax import lax
from jax.experimental import pallas as pl
from jax.experimental.pallas import tpu as pltpu
from jax.sharding import PartitionSpec as P

NE = 128
NT = 4096
NF = 1024
IX = 512
IZ = 4
POS_HERE = 2
QUARTER = NT // 4
LOWEST = 64
CENTRES = 48
SPACING = 20
FIRST = LOWEST + 9
PAIRS = ((1, -1), (3, -3), (5, -5), (7, -7), (9, -9), (2, -2), (4, -4), (6, -6), (8, -8), (0, 10))
GROUPS = len(PAIRS)
HALF = GROUPS // 2
TILES = IX // 128
MESH = pl.DeviceIdType.MESH

wave_speed = 0.5
pixel_pitch = 0.25
depth_start = 20.0
probe_anchor = 32

EVEN = ((-9, -5, -1, 3, 7), (-7, -3, 1, 5, 9))
ODD = ((-8, -4, 0, 4, 8), (-6, -2, 2, 6, 10))


def group_of(offset):
    group = [offset in pair for pair in PAIRS].index(True)
    return group, CENTRES * PAIRS[group].index(offset)


def time_tables():
    samples = np.arange(QUARTER)
    centres = FIRST + SPACING * np.arange(CENTRES)

    def parts(offsets):
        bins = np.concatenate([centres + offset for offset in offsets])
        angle = 2.0 * np.pi * (bins[:, None] * samples[None, :] % NT) / NT
        return np.cos(angle), -np.sin(angle)

    even = np.stack([np.concatenate(parts(offsets), axis=0) for offsets in EVEN])
    re1, im1 = parts(ODD[0])
    re3, im3 = parts(ODD[1])
    odd = np.concatenate(
        [np.concatenate([re1, im1], axis=1), np.concatenate([im3, re3], axis=1)], axis=0
    )
    return even.astype(ml_dtypes.bfloat16), odd.astype(ml_dtypes.bfloat16)


def element_table():
    pos = np.arange(NE) - (NE - 1) / 2.0
    angle = pos[:, None] * (np.arange(NE) - NE // 2)[None, :] * (2.0 * np.pi / NE)
    c, s = np.cos(angle), np.sin(angle)
    table = np.concatenate([np.concatenate([c, -s], axis=1), np.concatenate([s, c], axis=1)], axis=0)
    return table.astype(ml_dtypes.bfloat16)


def column_table():
    order = np.arange(NE) - NE // 2
    angle = 2.0 * np.pi * (order[:, None] * np.arange(IX)[None, :] % IX) / IX
    cosine, sine = np.cos(angle), np.sin(angle)
    tiles = []
    for start in range(0, IX, 128):
        c, s = cosine[:, start : start + 128], sine[:, start : start + 128]
        tiles.append(
            np.concatenate([np.concatenate([c, s], axis=1), np.concatenate([-s, c], axis=1)], axis=0)
        )
    return np.stack(tiles).astype(ml_dtypes.bfloat16)


def depth_table():
    centres = FIRST + SPACING * np.arange(CENTRES)
    wavenumber = (np.arange(NE) - NE // 2) * (2.0 * np.pi / NE)

    def parts(offset):
        k = (centres + offset)[:, None] * (2.0 * np.pi / NT) / wave_speed
        vertical = np.sqrt(np.maximum(k * k - wavenumber[None, :] ** 2, 0.0))
        weight = vertical / k
        first = weight * np.exp(1j * vertical * depth_start)
        step = np.exp(1j * vertical * pixel_pitch)
        return np.stack([first.real, first.imag, step.real, step.imag])

    groups = [
        np.concatenate([parts(offset) for offset in pair], axis=1) for pair in PAIRS
    ]
    return np.stack(groups, axis=1).astype(np.float32)


def turn_pair(turns):
    x = turns - jnp.floor(turns + 0.5)
    square = x * x
    sine = jnp.full_like(x, math.pi**13 / math.factorial(13))
    for power in (11, 9, 7, 5, 3, 1):
        sign = 1.0 if power % 4 == 1 else -1.0
        sine = sine * square + sign * math.pi**power / math.factorial(power)
    sine = sine * x
    cosine = jnp.full_like(x, math.pi**12 / math.factorial(12))
    for power in (10, 8, 6, 4, 2, 0):
        sign = 1.0 if power % 4 == 0 else -1.0
        cosine = cosine * square + sign * math.pi**power / math.factorial(power)
    return 1.0 - 2.0 * sine * sine, 2.0 * sine * cosine


def transposed_dot(a, b):
    return lax.dot_general(a, b, (((1,), (1,)), ((), ())), preferred_element_type=jnp.float32)


def hops(count, delta):
    return min(delta, count - delta)


PLANE = sorted(
    [(dy, dx) for dy in range(4) for dx in range(4) if dy or dx],
    key=lambda d: -(hops(4, d[0]) + hops(4, d[1])),
)
PENCIL = sorted(
    [(dz, dc) for dz in range(8) for dc in range(2) if dz or dc],
    key=lambda d: -(2 * hops(8, d[0]) + d[1]),
)


def focus_kernel(
    probe_ref, bins_ref, raw_hbm, even_hbm, odd_hbm, element_hbm, column_hbm, depth_hbm,
    out_ref,
    raw_ref, even_ref, odd_ref, element_ref, column_ref, depth_ref, loaded,
    negative, spectra, rows, counts, near, far, image,
    partial, inbox, middle, inbox2, send, recv, send2, recv2,
):
    section, freq, core = lax.axis_index("section"), lax.axis_index("freq"), lax.axis_index("pos")
    y, x_chip, z_chip = section * 2 + (freq >> 5), (freq >> 3) & 3, freq & 7

    def plane_device(dy, dx):
        yy, xx = (y + dy) & 3, (x_chip + dx) & 3
        return (yy >> 1, (yy & 1) * 32 + xx * 8 + z_chip, core)

    def pencil_device(dz, dc):
        return (section, (freq & 56) + ((z_chip + dz) & 7), (core + dc) & 1)

    def pieces(first, source, target, count):
        step = source.shape[0] // count
        return [
            pltpu.make_async_copy(
                source.at[pl.ds(i * step, step)], target.at[pl.ds(i * step, step)], loaded.at[first + i]
            )
            for i in range(count)
        ]

    raw_loads = pieces(0, raw_hbm, raw_ref, 4)
    even_loads = [pieces(4 + 2 * i, even_hbm.at[i], even_ref.at[i], 2) for i in range(2)]
    odd_loads = pieces(8, odd_hbm, odd_ref, 2)
    filter_loads = pieces(10, element_hbm, element_ref, 1) + pieces(11, depth_hbm, depth_ref, 4)
    column_loads = pieces(15, column_hbm, column_ref, 1)
    for copy in raw_loads + even_loads[0]:
        copy.start()

    barrier = pltpu.get_barrier_semaphore()
    for step in PLANE:
        pl.semaphore_signal(barrier, inc=1, device_id=plane_device(*step), device_id_type=MESH)
    for step in PENCIL:
        pl.semaphore_signal(barrier, inc=1, device_id=pencil_device(*step), device_id_type=MESH)

    bins = bins_ref[...] - LOWEST
    centre = (bins * 3277) >> 16
    offset = bins - SPACING * centre
    is_centre = jnp.where(lax.broadcasted_iota(jnp.int32, (CENTRES, NF), 0) == centre, 1.0, 0.0)
    is_offset = jnp.where(lax.broadcasted_iota(jnp.int32, (32, NF), 0) == offset, 1.0, 0.0)
    counts[...] = transposed_dot(is_centre.astype(jnp.bfloat16), is_offset.astype(jnp.bfloat16))

    tx_coord = (section * 64 + freq).astype(jnp.float32) - (NE - 1) / 2.0
    sub = lax.broadcasted_iota(jnp.int32, (16, 128), 0).astype(jnp.float32)
    near_powers = jnp.where(sub < 10.0, sub + 1.0, SPACING * 8.0)
    far_powers = FIRST + SPACING * sub[:8]
    lane = lax.broadcasted_iota(jnp.int32, (8, 128), 1)
    for p in range(POS_HERE):
        shift = 4 * (probe_ref[p] + probe_anchor)
        centre_here = (probe_ref[p] + probe_anchor).astype(jnp.float32)
        for tile in range(TILES):
            column = ((lane + (128 * tile + shift)) & (IX - 1)).astype(jnp.float32)
            x = (pixel_pitch * column - centre_here) - tx_coord
            for k in range(IZ):
                z = depth_start + pixel_pitch * k
                turns = jnp.sqrt(x * x + z * z) * (1.0 / (NT * wave_speed))
                c, s = turn_pair(jnp.concatenate([turns, turns], axis=0) * near_powers)
                near[tile, p * IZ + k, 0], near[tile, p * IZ + k, 1] = c, s
                c, s = turn_pair(turns * far_powers)
                far[tile, p * IZ + k, 0], far[tile, p * IZ + k, 1] = c, s

    def quarters(signs):
        return jnp.concatenate(
            [
                (raw_ref if sign > 0 else negative)[:, q * QUARTER : (q + 1) * QUARTER]
                for q, sign in enumerate(signs)
            ],
            axis=1,
        )

    def keep(values, offsets, part):
        for index, offset in enumerate(offsets):
            group, row = group_of(offset)
            for p in range(POS_HERE):
                spectra[p, group, row : row + CENTRES, part * NE : (part + 1) * NE] = values[
                    index * CENTRES : (index + 1) * CENTRES, p * NE : (p + 1) * NE
                ]

    def filtered(start, p):
        groups = range(start, start + HALF)
        fields = spectra[p, start : start + HALF].reshape(HALF * 2 * CENTRES, 2 * NE)
        fields = jnp.dot(fields, element_ref[...], preferred_element_type=jnp.float32)
        fields = fields.astype(jnp.bfloat16)
        for group in groups:
            scales = [counts[:, 9 + o : 10 + o] for o in PAIRS[group]]
            for block in range(0, CENTRES, 16):
                parts = []
                for half in range(2):
                    row = half * CENTRES + block
                    at = slice(row, row + 16)
                    field = fields[(group - start) * 2 * CENTRES + row :][:16].astype(jnp.float32)
                    scale = scales[half][block : block + 16]
                    re, im = field[:, :NE] * scale, field[:, NE:] * scale
                    cosine, sine = depth_ref[0, group, at, :], depth_ref[1, group, at, :]
                    parts.append([re * cosine - im * sine, re * sine + im * cosine])
                for k in range(IZ):
                    if k > 0:
                        for half in range(2):
                            at = slice(half * CENTRES + block, half * CENTRES + block + 16)
                            cosine, sine = depth_ref[2, group, at, :], depth_ref[3, group, at, :]
                            re, im = parts[half]
                            parts[half] = [re * cosine - im * sine, re * sine + im * cosine]
                    (re, im), (re_low, im_low) = parts
                    if group < GROUPS - 1:
                        values = (re + re_low, im + im_low, re - re_low, im - im_low)
                    else:
                        values = (re, im, re_low, im_low)
                    re, im, re_low, im_low = [value.astype(jnp.bfloat16) for value in values]
                    top = slice(block, block + 16)
                    low = slice(CENTRES + block, CENTRES + block + 16)
                    rows[p * IZ + k, group, top, :NE] = re
                    rows[p * IZ + k, group, top, NE:] = im
                    rows[p * IZ + k, group, low, :NE] = re_low
                    rows[p * IZ + k, group, low, NE:] = im_low

    half_rows = 5 * CENTRES
    left, right = slice(0, QUARTER), slice(QUARTER, 2 * QUARTER)

    def even_bins(index):
        table = even_ref[index]
        signs = (1, 1 - 2 * index, 1, 1 - 2 * index)
        out = transposed_dot(jnp.concatenate([table] * 4, axis=1), quarters(signs)).astype(jnp.bfloat16)
        keep(out[:half_rows], EVEN[index], 0)
        keep(out[half_rows:], EVEN[index], 1)

    def odd_bins(index):
        one, two = odd_ref[:, (left, right)[index]], odd_ref[:, (right, left)[index]]
        signs = ((1, 1, -1, -1), (1, -1, -1, 1))[index]
        out = transposed_dot(
            jnp.concatenate([one, two, one, two], axis=1), quarters(signs)
        ).astype(jnp.bfloat16)
        keep(out[:half_rows], ODD[0], index)
        keep(out[half_rows:], ODD[1], 1 - index)

    for copy in even_loads[1]:
        copy.start()
    for copy in raw_loads + even_loads[0] + even_loads[1]:
        copy.wait()
    for copy in odd_loads + filter_loads + column_loads:
        copy.start()
    even_bins(0)
    for q in range(1, 4):
        negative[:, q * QUARTER : (q + 1) * QUARTER] = -raw_ref[:, q * QUARTER : (q + 1) * QUARTER]
    even_bins(1)
    for copy in odd_loads + filter_loads + column_loads:
        copy.wait()
    filtered(0, 0)
    odd_bins(0)
    filtered(0, 1)
    odd_bins(1)
    filtered(HALF, 0)
    filtered(HALF, 1)

    @pl.loop(0, TILES, unroll=TILES)
    def _(tile):
        weights = column_ref[tile]
        for pk in range(POS_HERE * IZ):
            total_re = jnp.zeros((CENTRES, 128), jnp.float32)
            total_im = jnp.zeros((CENTRES, 128), jnp.float32)
            several = rows[pk].reshape(GROUPS * 2 * CENTRES, 2 * NE)
            several = jnp.dot(several, weights, preferred_element_type=jnp.float32)
            for group, (offset, other) in enumerate(PAIRS):
                first = group * 2 * CENTRES
                both = several[first : first + 2 * CENTRES]
                power = max(offset, other)
                c, s = near[tile, pk, 0, power - 1 : power, :], near[tile, pk, 1, power - 1 : power, :]
                low_re, low_im = both[CENTRES:, :128], both[CENTRES:, 128:]
                if group < GROUPS - 1:
                    total_re += c * both[:CENTRES, :128] - s * low_im
                    total_im += c * both[:CENTRES, 128:] + s * low_re
                else:
                    total_re += both[:CENTRES, :128] + (c * low_re - s * low_im)
                    total_im += both[:CENTRES, 128:] + (c * low_im + s * low_re)
            jump_cos = jnp.broadcast_to(near[tile, pk, 0, 10:11, :], (8, 128))
            jump_sin = jnp.broadcast_to(near[tile, pk, 1, 10:11, :], (8, 128))
            re, im = total_re[CENTRES - 8 :], total_im[CENTRES - 8 :]
            for g in range(CENTRES // 8 - 2, -1, -1):
                re, im = (
                    re * jump_cos - im * jump_sin + total_re[8 * g : 8 * g + 8],
                    re * jump_sin + im * jump_cos + total_im[8 * g : 8 * g + 8],
                )
            value = re * far[tile, pk, 0] - im * far[tile, pk, 1]
            image[tile, pk : pk + 1, :] = jnp.sum(value, axis=0, keepdims=True)

    both = jnp.concatenate([image[tile] for tile in range(TILES)], axis=1)
    is_first = lax.broadcasted_iota(jnp.int32, (POS_HERE * IZ, IX), 0) < IZ
    turn = jnp.where(is_first, probe_ref[0] + probe_anchor, probe_ref[1] + probe_anchor)
    for bit in range(7):
        both = jnp.where(((turn >> bit) & 1) == 1, pltpu.roll(both, 4 << bit, 1), both)
    scale = 1.0 / math.sqrt(float(NT * NE**3 * NF * 4))
    for tile in range(TILES):
        columns = slice(tile * 128, (tile + 1) * 128)
        partial[tile] = (both[:IZ, columns] + both[IZ:, columns]) * scale

    pl.semaphore_wait(barrier, len(PLANE) + len(PENCIL))
    copies = []
    for index, step in enumerate(PLANE):
        copy = pltpu.make_async_remote_copy(
            src_ref=partial.at[(y + step[0]) & 3],
            dst_ref=inbox.at[index],
            send_sem=send.at[index],
            recv_sem=recv.at[index],
            device_id=plane_device(*step),
            device_id_type=MESH,
        )
        copy.start()
        copies.append(copy)
    total = partial[y]
    for index in reversed(range(len(PLANE))):
        copies[index].wait_recv()
        total = total + inbox[index]
    middle[...] = total
    copies2 = []
    for index, step in enumerate(PENCIL):
        copy = pltpu.make_async_remote_copy(
            src_ref=middle,
            dst_ref=inbox2.at[index],
            send_sem=send2.at[index],
            recv_sem=recv2.at[index],
            device_id=pencil_device(*step),
            device_id_type=MESH,
        )
        copy.start()
        copies2.append(copy)
    for index in reversed(range(len(PENCIL))):
        copies2[index].wait_recv()
        total = total + inbox2[index]
    out_ref[...] = pltpu.roll(total, (128 - (x_chip * 32 + z_chip * 4)) & 127, 1)
    for copy in copies + copies2:
        copy.wait_send()


def focus(raw, band_bins, probe_index):
    even, odd = time_tables()
    tables = [even, odd, element_table(), column_table(), depth_table()]
    vmem = pl.BlockSpec(memory_space=pltpu.VMEM)
    smem = pl.BlockSpec(memory_space=pltpu.SMEM)
    hbm = pl.BlockSpec(memory_space=pltpu.HBM)
    held = [pltpu.VMEM((POS_HERE * NE, NT), jnp.bfloat16)]
    held += [pltpu.VMEM(table.shape, table.dtype) for table in tables]
    tile = (IZ, 128)
    return pl.pallas_call(
        focus_kernel,
        out_shape=jax.ShapeDtypeStruct(tile, jnp.float32),
        in_specs=[smem, vmem] + [hbm] * 6,
        out_specs=vmem,
        scratch_shapes=[
            *held,
            pltpu.SemaphoreType.DMA((16,)),
            pltpu.VMEM((POS_HERE * NE, NT), jnp.bfloat16),
            pltpu.VMEM((POS_HERE, GROUPS, 2 * CENTRES, 2 * NE), jnp.bfloat16),
            pltpu.VMEM((POS_HERE * IZ, GROUPS, 2 * CENTRES, 2 * NE), jnp.bfloat16),
            pltpu.VMEM((CENTRES, 32), jnp.float32),
            pltpu.VMEM((TILES, POS_HERE * IZ, 2, 16, 128), jnp.float32),
            pltpu.VMEM((TILES, POS_HERE * IZ, 2, 8, 128), jnp.float32),
            pltpu.VMEM((TILES, POS_HERE * IZ, 128), jnp.float32),
            pltpu.VMEM((TILES, *tile), jnp.float32),
            pltpu.VMEM((15, *tile), jnp.float32),
            pltpu.VMEM(tile, jnp.float32),
            pltpu.VMEM((15, *tile), jnp.float32),
            pltpu.SemaphoreType.DMA((15,)),
            pltpu.SemaphoreType.DMA((15,)),
            pltpu.SemaphoreType.DMA((15,)),
            pltpu.SemaphoreType.DMA((15,)),
        ],
        compiler_params=pltpu.CompilerParams(
            collective_id=0, has_side_effects=True, vmem_limit_bytes=63 * 1024 * 1024
        ),
        name="focus",
    )(
        probe_index,
        band_bins.reshape(1, NF),
        raw.reshape(POS_HERE * NE, NT),
        *[jnp.asarray(table) for table in tables],
    )


def per_device(raw_capture, band_bins, probe_index):
    return focus(raw_capture, band_bins, probe_index)[:, :4]


def solution(mesh):
    in_specs = (P("pos", ("section", "freq"), None, None), P(), P("pos"))
    out_specs = P(None, ("section", "freq"))
    return jax.shard_map(
        per_device, mesh=mesh, in_specs=in_specs, out_specs=out_specs, check_vma=False
    )
```

```python
import math

import jax
import jax.numpy as jnp
import ml_dtypes
import numpy as np
from jax import lax
from jax.experimental import pallas as pl
from jax.experimental.pallas import tpu as pltpu
from jax.sharding import PartitionSpec as P

NE = 128
NT = 4096
NF = 1024
IX = 512
IZ = 4
POS_HERE = 2
QUARTER = NT // 4
LOWEST = 64
CENTRES = 48
SPACING = 20
FIRST = LOWEST + 9
PAIRS = ((1, -1), (3, -3), (5, -5), (7, -7), (9, -9), (2, -2), (4, -4), (6, -6), (8, -8), (0, 10))
GROUPS = len(PAIRS)
HALF = GROUPS // 2
TILES = IX // 128
MESH = pl.DeviceIdType.MESH

wave_speed = 0.5
pixel_pitch = 0.25
depth_start = 20.0
probe_anchor = 32

EVEN = ((-9, -5, -1, 3, 7), (-7, -3, 1, 5, 9))
ODD = ((-8, -4, 0, 4, 8), (-6, -2, 2, 6, 10))


def group_of(offset):
    group = [offset in pair for pair in PAIRS].index(True)
    return group, CENTRES * PAIRS[group].index(offset)


def time_tables():
    samples = np.arange(QUARTER)
    centres = FIRST + SPACING * np.arange(CENTRES)

    def parts(offsets):
        bins = np.concatenate([centres + offset for offset in offsets])
        angle = 2.0 * np.pi * (bins[:, None] * samples[None, :] % NT) / NT
        return np.cos(angle), -np.sin(angle)

    even = np.stack([np.concatenate(parts(offsets), axis=0) for offsets in EVEN])
    re1, im1 = parts(ODD[0])
    re3, im3 = parts(ODD[1])
    odd = np.concatenate(
        [np.concatenate([re1, im1], axis=1), np.concatenate([im3, re3], axis=1)], axis=0
    )
    return even.astype(ml_dtypes.bfloat16), odd.astype(ml_dtypes.bfloat16)


def element_table():
    pos = np.arange(NE) - (NE - 1) / 2.0
    angle = pos[:, None] * (np.arange(NE) - NE // 2)[None, :] * (2.0 * np.pi / NE)
    c, s = np.cos(angle), np.sin(angle)
    table = np.concatenate([np.concatenate([c, -s], axis=1), np.concatenate([s, c], axis=1)], axis=0)
    return table.astype(ml_dtypes.bfloat16)


def column_table():
    order = np.arange(NE) - NE // 2
    angle = 2.0 * np.pi * (order[:, None] * np.arange(IX)[None, :] % IX) / IX
    cosine, sine = np.cos(angle), np.sin(angle)
    tiles = []
    for start in range(0, IX, 128):
        c, s = cosine[:, start : start + 128], sine[:, start : start + 128]
        tiles.append(
            np.concatenate([np.concatenate([c, s], axis=1), np.concatenate([-s, c], axis=1)], axis=0)
        )
    return np.stack(tiles).astype(ml_dtypes.bfloat16)


def depth_table():
    centres = FIRST + SPACING * np.arange(CENTRES)
    wavenumber = (np.arange(NE) - NE // 2) * (2.0 * np.pi / NE)

    def parts(offset):
        k = (centres + offset)[:, None] * (2.0 * np.pi / NT) / wave_speed
        vertical = np.sqrt(np.maximum(k * k - wavenumber[None, :] ** 2, 0.0))
        weight = vertical / k
        first = weight * np.exp(1j * vertical * depth_start)
        step = np.exp(1j * vertical * pixel_pitch)
        return np.stack([first.real, first.imag, step.real, step.imag])

    groups = [
        np.concatenate([parts(offset) for offset in pair], axis=1) for pair in PAIRS
    ]
    return np.stack(groups, axis=1).astype(np.float32)


def turn_pair(turns):
    x = turns - jnp.floor(turns + 0.5)
    square = x * x
    sine = jnp.full_like(x, math.pi**13 / math.factorial(13))
    for power in (11, 9, 7, 5, 3, 1):
        sign = 1.0 if power % 4 == 1 else -1.0
        sine = sine * square + sign * math.pi**power / math.factorial(power)
    sine = sine * x
    cosine = jnp.full_like(x, math.pi**12 / math.factorial(12))
    for power in (10, 8, 6, 4, 2, 0):
        sign = 1.0 if power % 4 == 0 else -1.0
        cosine = cosine * square + sign * math.pi**power / math.factorial(power)
    return 1.0 - 2.0 * sine * sine, 2.0 * sine * cosine


def transposed_dot(a, b):
    return lax.dot_general(a, b, (((1,), (1,)), ((), ())), preferred_element_type=jnp.float32)


def hops(count, delta):
    return min(delta, count - delta)


PLANE = sorted(
    [(dy, dx) for dy in range(4) for dx in range(4) if dy or dx],
    key=lambda d: -(hops(4, d[0]) + hops(4, d[1])),
)
PENCIL = sorted(
    [(dz, dc) for dz in range(8) for dc in range(2) if dz or dc],
    key=lambda d: -(2 * hops(8, d[0]) + d[1]),
)


def focus_kernel(
    probe_ref, bins_ref, raw_hbm, even_hbm, odd_hbm, element_hbm, column_hbm, depth_hbm,
    out_ref,
    raw_ref, even_ref, odd_ref, element_ref, column_ref, depth_ref, loaded,
    negative, spectra, rows, counts, near, far, image,
    partial, inbox, middle, inbox2, send, recv, send2, recv2,
):
    section, freq, core = lax.axis_index("section"), lax.axis_index("freq"), lax.axis_index("pos")
    y, x_chip, z_chip = section * 2 + (freq >> 5), (freq >> 3) & 3, freq & 7

    def plane_device(dy, dx):
        yy, xx = (y + dy) & 3, (x_chip + dx) & 3
        return (yy >> 1, (yy & 1) * 32 + xx * 8 + z_chip, core)

    def pencil_device(dz, dc):
        return (section, (freq & 56) + ((z_chip + dz) & 7), (core + dc) & 1)

    def pieces(first, source, target, count):
        step = source.shape[0] // count
        return [
            pltpu.make_async_copy(
                source.at[pl.ds(i * step, step)], target.at[pl.ds(i * step, step)], loaded.at[first + i]
            )
            for i in range(count)
        ]

    raw_loads = pieces(0, raw_hbm, raw_ref, 4)
    even_loads = [pieces(4 + 2 * i, even_hbm.at[i], even_ref.at[i], 2) for i in range(2)]
    odd_loads = pieces(8, odd_hbm, odd_ref, 2)
    filter_loads = pieces(10, element_hbm, element_ref, 1) + pieces(11, depth_hbm, depth_ref, 4)
    column_loads = pieces(15, column_hbm, column_ref, 1)
    for copy in raw_loads + even_loads[0] + even_loads[1]:
        copy.start()

    barrier = pltpu.get_barrier_semaphore()
    for step in PLANE:
        pl.semaphore_signal(barrier, inc=1, device_id=plane_device(*step), device_id_type=MESH)
    for step in PENCIL:
        pl.semaphore_signal(barrier, inc=1, device_id=pencil_device(*step), device_id_type=MESH)

    bins = bins_ref[...] - LOWEST
    centre = (bins * 3277) >> 16
    offset = bins - SPACING * centre
    is_centre = jnp.where(lax.broadcasted_iota(jnp.int32, (CENTRES, NF), 0) == centre, 1.0, 0.0)
    is_offset = jnp.where(lax.broadcasted_iota(jnp.int32, (32, NF), 0) == offset, 1.0, 0.0)
    counts[...] = transposed_dot(is_centre.astype(jnp.bfloat16), is_offset.astype(jnp.bfloat16))

    tx_coord = (section * 64 + freq).astype(jnp.float32) - (NE - 1) / 2.0
    sub = lax.broadcasted_iota(jnp.int32, (16, 128), 0).astype(jnp.float32)
    near_powers = jnp.where(sub < 10.0, sub + 1.0, SPACING * 8.0)
    far_powers = FIRST + SPACING * sub[:8]
    lane = lax.broadcasted_iota(jnp.int32, (8, 128), 1)
    for p in range(POS_HERE):
        shift = 4 * (probe_ref[p] + probe_anchor)
        centre_here = (probe_ref[p] + probe_anchor).astype(jnp.float32)
        for tile in range(TILES):
            column = ((lane + (128 * tile + shift)) & (IX - 1)).astype(jnp.float32)
            x = (pixel_pitch * column - centre_here) - tx_coord
            for k in range(IZ):
                z = depth_start + pixel_pitch * k
                turns = jnp.sqrt(x * x + z * z) * (1.0 / (NT * wave_speed))
                c, s = turn_pair(jnp.concatenate([turns, turns], axis=0) * near_powers)
                near[tile, p * IZ + k, 0], near[tile, p * IZ + k, 1] = c, s
                c, s = turn_pair(turns * far_powers)
                far[tile, p * IZ + k, 0], far[tile, p * IZ + k, 1] = c, s

    def quarters(signs):
        return jnp.concatenate(
            [
                (raw_ref if sign > 0 else negative)[:, q * QUARTER : (q + 1) * QUARTER]
                for q, sign in enumerate(signs)
            ],
            axis=1,
        )

    def keep(values, offsets, part):
        for index, offset in enumerate(offsets):
            group, row = group_of(offset)
            for p in range(POS_HERE):
                spectra[p, group, row : row + CENTRES, part * NE : (part + 1) * NE] = values[
                    index * CENTRES : (index + 1) * CENTRES, p * NE : (p + 1) * NE
                ]

    def filtered(start, p):
        groups = range(start, start + HALF)
        fields = spectra[p, start : start + HALF].reshape(HALF * 2 * CENTRES, 2 * NE)
        fields = jnp.dot(fields, element_ref[...], preferred_element_type=jnp.float32)
        fields = fields.astype(jnp.bfloat16)
        for group in groups:
            scales = [counts[:, 9 + o : 10 + o] for o in PAIRS[group]]
            for block in range(0, CENTRES, 16):
                parts = []
                for half in range(2):
                    row = half * CENTRES + block
                    at = slice(row, row + 16)
                    field = fields[(group - start) * 2 * CENTRES + row :][:16].astype(jnp.float32)
                    scale = scales[half][block : block + 16]
                    re, im = field[:, :NE] * scale, field[:, NE:] * scale
                    cosine, sine = depth_ref[0, group, at, :], depth_ref[1, group, at, :]
                    parts.append([re * cosine - im * sine, re * sine + im * cosine])
                for k in range(IZ):
                    if k > 0:
                        for half in range(2):
                            at = slice(half * CENTRES + block, half * CENTRES + block + 16)
                            cosine, sine = depth_ref[2, group, at, :], depth_ref[3, group, at, :]
                            re, im = parts[half]
                            parts[half] = [re * cosine - im * sine, re * sine + im * cosine]
                    (re, im), (re_low, im_low) = parts
                    if group < GROUPS - 1:
                        values = (re + re_low, im + im_low, re - re_low, im - im_low)
                    else:
                        values = (re, im, re_low, im_low)
                    re, im, re_low, im_low = [value.astype(jnp.bfloat16) for value in values]
                    top = slice(block, block + 16)
                    low = slice(CENTRES + block, CENTRES + block + 16)
                    rows[p * IZ + k, group, top, :NE] = re
                    rows[p * IZ + k, group, top, NE:] = im
                    rows[p * IZ + k, group, low, :NE] = re_low
                    rows[p * IZ + k, group, low, NE:] = im_low

    half_rows = 5 * CENTRES
    left, right = slice(0, QUARTER), slice(QUARTER, 2 * QUARTER)

    def even_bins(index):
        table = even_ref[index]
        signs = (1, 1 - 2 * index, 1, 1 - 2 * index)
        out = transposed_dot(jnp.concatenate([table] * 4, axis=1), quarters(signs)).astype(jnp.bfloat16)
        keep(out[:half_rows], EVEN[index], 0)
        keep(out[half_rows:], EVEN[index], 1)

    def odd_bins(index):
        one, two = odd_ref[:, (left, right)[index]], odd_ref[:, (right, left)[index]]
        signs = ((1, 1, -1, -1), (1, -1, -1, 1))[index]
        out = transposed_dot(
            jnp.concatenate([one, two, one, two], axis=1), quarters(signs)
        ).astype(jnp.bfloat16)
        keep(out[:half_rows], ODD[0], index)
        keep(out[half_rows:], ODD[1], 1 - index)

    for copy in raw_loads + even_loads[0] + even_loads[1]:
        copy.wait()
    for copy in odd_loads + filter_loads + column_loads:
        copy.start()
    even_bins(0)
    for q in range(1, 4):
        negative[:, q * QUARTER : (q + 1) * QUARTER] = -raw_ref[:, q * QUARTER : (q + 1) * QUARTER]
    even_bins(1)
    for copy in odd_loads + filter_loads + column_loads:
        copy.wait()
    filtered(0, 0)
    odd_bins(0)
    filtered(0, 1)
    odd_bins(1)
    filtered(HALF, 0)
    filtered(HALF, 1)

    @pl.loop(0, TILES, unroll=TILES)
    def _(tile):
        weights = column_ref[tile]
        for pk in range(POS_HERE * IZ):
            total_re = jnp.zeros((CENTRES, 128), jnp.float32)
            total_im = jnp.zeros((CENTRES, 128), jnp.float32)
            several = rows[pk].reshape(GROUPS * 2 * CENTRES, 2 * NE)
            several = jnp.dot(several, weights, preferred_element_type=jnp.float32)
            for group, (offset, other) in enumerate(PAIRS):
                first = group * 2 * CENTRES
                both = several[first : first + 2 * CENTRES]
                power = max(offset, other)
                c, s = near[tile, pk, 0, power - 1 : power, :], near[tile, pk, 1, power - 1 : power, :]
                low_re, low_im = both[CENTRES:, :128], both[CENTRES:, 128:]
                if group < GROUPS - 1:
                    total_re += c * both[:CENTRES, :128] - s * low_im
                    total_im += c * both[:CENTRES, 128:] + s * low_re
                else:
                    total_re += both[:CENTRES, :128] + (c * low_re - s * low_im)
                    total_im += both[:CENTRES, 128:] + (c * low_im + s * low_re)
            jump_cos = jnp.broadcast_to(near[tile, pk, 0, 10:11, :], (8, 128))
            jump_sin = jnp.broadcast_to(near[tile, pk, 1, 10:11, :], (8, 128))
            re, im = total_re[CENTRES - 8 :], total_im[CENTRES - 8 :]
            for g in range(CENTRES // 8 - 2, -1, -1):
                re, im = (
                    re * jump_cos - im * jump_sin + total_re[8 * g : 8 * g + 8],
                    re * jump_sin + im * jump_cos + total_im[8 * g : 8 * g + 8],
                )
            value = re * far[tile, pk, 0] - im * far[tile, pk, 1]
            image[tile, pk : pk + 1, :] = jnp.sum(value, axis=0, keepdims=True)

    both = jnp.concatenate([image[tile] for tile in range(TILES)], axis=1)
    is_first = lax.broadcasted_iota(jnp.int32, (POS_HERE * IZ, IX), 0) < IZ
    turn = jnp.where(is_first, probe_ref[0] + probe_anchor, probe_ref[1] + probe_anchor)
    for bit in range(7):
        both = jnp.where(((turn >> bit) & 1) == 1, pltpu.roll(both, 4 << bit, 1), both)
    scale = 1.0 / math.sqrt(float(NT * NE**3 * NF * 4))
    for tile in range(TILES):
        columns = slice(tile * 128, (tile + 1) * 128)
        partial[tile] = (both[:IZ, columns] + both[IZ:, columns]) * scale

    pl.semaphore_wait(barrier, len(PLANE) + len(PENCIL))
    for index, step in enumerate(PLANE):
        copy = pltpu.make_async_remote_copy(
            src_ref=partial.at[(y + step[0]) & 3],
            dst_ref=inbox.at[index],
            send_sem=send,
            recv_sem=recv,
            device_id=plane_device(*step),
            device_id_type=MESH,
        )
        copy.start()
    pltpu.make_async_copy(inbox, inbox, recv).wait()
    total = partial[y] + jnp.sum(inbox[...], axis=0)
    middle[...] = total
    for index, step in enumerate(PENCIL):
        copy = pltpu.make_async_remote_copy(
            src_ref=middle,
            dst_ref=inbox2.at[index],
            send_sem=send2,
            recv_sem=recv2,
            device_id=pencil_device(*step),
            device_id_type=MESH,
        )
        copy.start()
    pltpu.make_async_copy(inbox2, inbox2, recv2).wait()
    total = total + jnp.sum(inbox2[...], axis=0)
    out_ref[...] = pltpu.roll(total, (128 - (x_chip * 32 + z_chip * 4)) & 127, 1)
    pltpu.make_async_copy(inbox, inbox, send).wait()
    pltpu.make_async_copy(inbox2, inbox2, send2).wait()


def focus(raw, band_bins, probe_index):
    even, odd = time_tables()
    tables = [even, odd, element_table(), column_table(), depth_table()]
    vmem = pl.BlockSpec(memory_space=pltpu.VMEM)
    smem = pl.BlockSpec(memory_space=pltpu.SMEM)
    hbm = pl.BlockSpec(memory_space=pltpu.HBM)
    held = [pltpu.VMEM((POS_HERE * NE, NT), jnp.bfloat16)]
    held += [pltpu.VMEM(table.shape, table.dtype) for table in tables]
    tile = (IZ, 128)
    return pl.pallas_call(
        focus_kernel,
        out_shape=jax.ShapeDtypeStruct(tile, jnp.float32),
        in_specs=[smem, vmem] + [hbm] * 6,
        out_specs=vmem,
        scratch_shapes=[
            *held,
            pltpu.SemaphoreType.DMA((16,)),
            pltpu.VMEM((POS_HERE * NE, NT), jnp.bfloat16),
            pltpu.VMEM((POS_HERE, GROUPS, 2 * CENTRES, 2 * NE), jnp.bfloat16),
            pltpu.VMEM((POS_HERE * IZ, GROUPS, 2 * CENTRES, 2 * NE), jnp.bfloat16),
            pltpu.VMEM((CENTRES, 32), jnp.float32),
            pltpu.VMEM((TILES, POS_HERE * IZ, 2, 16, 128), jnp.float32),
            pltpu.VMEM((TILES, POS_HERE * IZ, 2, 8, 128), jnp.float32),
            pltpu.VMEM((TILES, POS_HERE * IZ, 128), jnp.float32),
            pltpu.VMEM((TILES, *tile), jnp.float32),
            pltpu.VMEM((15, *tile), jnp.float32),
            pltpu.VMEM(tile, jnp.float32),
            pltpu.VMEM((15, *tile), jnp.float32),
            pltpu.SemaphoreType.DMA,
            pltpu.SemaphoreType.DMA,
            pltpu.SemaphoreType.DMA,
            pltpu.SemaphoreType.DMA,
        ],
        compiler_params=pltpu.CompilerParams(
            collective_id=0, has_side_effects=True, vmem_limit_bytes=63 * 1024 * 1024
        ),
        name="focus",
    )(
        probe_index,
        band_bins.reshape(1, NF),
        raw.reshape(POS_HERE * NE, NT),
        *[jnp.asarray(table) for table in tables],
    )


def per_device(raw_capture, band_bins, probe_index):
    return focus(raw_capture, band_bins, probe_index)[:, :4]


def solution(mesh):
    in_specs = (P("pos", ("section", "freq"), None, None), P(), P("pos"))
    out_specs = P(None, ("section", "freq"))
    return jax.shard_map(
        per_device, mesh=mesh, in_specs=in_specs, out_specs=out_specs, check_vma=False
    )
```

```python
import math

import jax
import jax.numpy as jnp
import ml_dtypes
import numpy as np
from jax import lax
from jax.experimental import pallas as pl
from jax.experimental.pallas import tpu as pltpu
from jax.sharding import PartitionSpec as P

NE = 128
NT = 4096
NF = 1024
IX = 512
IZ = 4
POS_HERE = 2
QUARTER = NT // 4
LOWEST = 64
CENTRES = 48
SPACING = 20
FIRST = LOWEST + 9
PAIRS = ((1, -1), (3, -3), (5, -5), (7, -7), (9, -9), (2, -2), (4, -4), (6, -6), (8, -8), (0, 10))
GROUPS = len(PAIRS)
HALF = GROUPS // 2
TILES = IX // 128
MESH = pl.DeviceIdType.MESH

wave_speed = 0.5
pixel_pitch = 0.25
depth_start = 20.0
probe_anchor = 32

EVEN = ((-9, -5, -1, 3, 7), (-7, -3, 1, 5, 9))
ODD = ((-8, -4, 0, 4, 8), (-6, -2, 2, 6, 10))


def group_of(offset):
    group = [offset in pair for pair in PAIRS].index(True)
    return group, CENTRES * PAIRS[group].index(offset)


def time_tables():
    samples = np.arange(QUARTER)
    centres = FIRST + SPACING * np.arange(CENTRES)

    def parts(offsets):
        bins = np.concatenate([centres + offset for offset in offsets])
        angle = 2.0 * np.pi * (bins[:, None] * samples[None, :] % NT) / NT
        return np.cos(angle), -np.sin(angle)

    even = np.stack([np.concatenate(parts(offsets), axis=0) for offsets in EVEN])
    re1, im1 = parts(ODD[0])
    re3, im3 = parts(ODD[1])
    odd = np.concatenate(
        [np.concatenate([re1, im1], axis=1), np.concatenate([im3, re3], axis=1)], axis=0
    )
    return even.astype(ml_dtypes.bfloat16), odd.astype(ml_dtypes.bfloat16)


def element_table():
    pos = np.arange(NE) - (NE - 1) / 2.0
    angle = pos[:, None] * (np.arange(NE) - NE // 2)[None, :] * (2.0 * np.pi / NE)
    c, s = np.cos(angle), np.sin(angle)
    table = np.concatenate([np.concatenate([c, -s], axis=1), np.concatenate([s, c], axis=1)], axis=0)
    return table.astype(ml_dtypes.bfloat16)


def column_table():
    order = np.arange(NE) - NE // 2
    angle = 2.0 * np.pi * (order[:, None] * np.arange(IX)[None, :] % IX) / IX
    cosine, sine = np.cos(angle), np.sin(angle)
    tiles = []
    for start in range(0, IX, 128):
        c, s = cosine[:, start : start + 128], sine[:, start : start + 128]
        tiles.append(
            np.concatenate([np.concatenate([c, s], axis=1), np.concatenate([-s, c], axis=1)], axis=0)
        )
    return np.stack(tiles).astype(ml_dtypes.bfloat16)


def depth_table():
    centres = FIRST + SPACING * np.arange(CENTRES)
    wavenumber = (np.arange(NE) - NE // 2) * (2.0 * np.pi / NE)

    def parts(offset):
        k = (centres + offset)[:, None] * (2.0 * np.pi / NT) / wave_speed
        vertical = np.sqrt(np.maximum(k * k - wavenumber[None, :] ** 2, 0.0))
        weight = vertical / k
        first = weight * np.exp(1j * vertical * depth_start)
        step = np.exp(1j * vertical * pixel_pitch)
        return np.stack([first.real, first.imag, step.real, step.imag])

    groups = [
        np.concatenate([parts(offset) for offset in pair], axis=1) for pair in PAIRS
    ]
    return np.stack(groups, axis=1).astype(np.float32)


def turn_pair(turns):
    x = turns - jnp.floor(turns + 0.5)
    square = x * x
    sine = jnp.full_like(x, math.pi**13 / math.factorial(13))
    for power in (11, 9, 7, 5, 3, 1):
        sign = 1.0 if power % 4 == 1 else -1.0
        sine = sine * square + sign * math.pi**power / math.factorial(power)
    sine = sine * x
    cosine = jnp.full_like(x, math.pi**12 / math.factorial(12))
    for power in (10, 8, 6, 4, 2, 0):
        sign = 1.0 if power % 4 == 0 else -1.0
        cosine = cosine * square + sign * math.pi**power / math.factorial(power)
    return 1.0 - 2.0 * sine * sine, 2.0 * sine * cosine


def transposed_dot(a, b):
    return lax.dot_general(a, b, (((1,), (1,)), ((), ())), preferred_element_type=jnp.float32)


def hops(count, delta):
    return min(delta, count - delta)


PLANE = sorted(
    [(dy, dx) for dy in range(4) for dx in range(4) if dy or dx],
    key=lambda d: -(hops(4, d[0]) + hops(4, d[1])),
)
PENCIL = sorted(
    [(dz, dc) for dz in range(8) for dc in range(2) if dz or dc],
    key=lambda d: -(2 * hops(8, d[0]) + d[1]),
)


def focus_kernel(
    probe_ref, bins_ref, raw_hbm, even_hbm, odd_hbm, element_hbm, column_hbm, depth_hbm,
    out_ref,
    raw_ref, even_ref, odd_ref, element_ref, column_ref, depth_ref, loaded,
    negative, spectra, rows, counts, near, far, image,
    partial, inbox, middle, inbox2, send, recv, send2, recv2,
):
    section, freq, core = lax.axis_index("section"), lax.axis_index("freq"), lax.axis_index("pos")
    y, x_chip, z_chip = section * 2 + (freq >> 5), (freq >> 3) & 3, freq & 7

    def plane_device(dy, dx):
        yy, xx = (y + dy) & 3, (x_chip + dx) & 3
        return (yy >> 1, (yy & 1) * 32 + xx * 8 + z_chip, core)

    def pencil_device(dz, dc):
        return (section, (freq & 56) + ((z_chip + dz) & 7), (core + dc) & 1)

    def pieces(first, source, target, count):
        step = source.shape[0] // count
        return [
            pltpu.make_async_copy(
                source.at[pl.ds(i * step, step)], target.at[pl.ds(i * step, step)], loaded.at[first + i]
            )
            for i in range(count)
        ]

    raw_loads = pieces(0, raw_hbm, raw_ref, 4)
    even_loads = [pieces(4 + 2 * i, even_hbm.at[i], even_ref.at[i], 2) for i in range(2)]
    odd_loads = pieces(8, odd_hbm, odd_ref, 2)
    filter_loads = pieces(10, element_hbm, element_ref, 1) + pieces(11, depth_hbm, depth_ref, 4)
    column_loads = pieces(15, column_hbm, column_ref, 1)
    for copy in raw_loads + even_loads[0] + even_loads[1]:
        copy.start()

    barrier = pltpu.get_barrier_semaphore()
    for step in PLANE:
        pl.semaphore_signal(barrier, inc=1, device_id=plane_device(*step), device_id_type=MESH)
    for step in PENCIL:
        pl.semaphore_signal(barrier, inc=1, device_id=pencil_device(*step), device_id_type=MESH)

    bins = bins_ref[...] - LOWEST
    centre = (bins * 3277) >> 16
    offset = bins - SPACING * centre
    is_centre = jnp.where(lax.broadcasted_iota(jnp.int32, (CENTRES, NF), 0) == centre, 1.0, 0.0)
    is_offset = jnp.where(lax.broadcasted_iota(jnp.int32, (32, NF), 0) == offset, 1.0, 0.0)
    counts[...] = transposed_dot(is_centre.astype(jnp.bfloat16), is_offset.astype(jnp.bfloat16))

    tx_coord = (section * 64 + freq).astype(jnp.float32) - (NE - 1) / 2.0
    sub = lax.broadcasted_iota(jnp.int32, (16, 128), 0).astype(jnp.float32)
    near_powers = jnp.where(sub < 10.0, sub + 1.0, SPACING * 8.0)
    far_powers = FIRST + SPACING * sub[:8]
    lane = lax.broadcasted_iota(jnp.int32, (8, 128), 1)
    for p in range(POS_HERE):
        shift = 4 * (probe_ref[p] + probe_anchor)
        centre_here = (probe_ref[p] + probe_anchor).astype(jnp.float32)
        for tile in range(TILES):
            column = ((lane + (128 * tile + shift)) & (IX - 1)).astype(jnp.float32)
            x = (pixel_pitch * column - centre_here) - tx_coord
            for k in range(IZ):
                z = depth_start + pixel_pitch * k
                turns = jnp.sqrt(x * x + z * z) * (1.0 / (NT * wave_speed))
                c, s = turn_pair(jnp.concatenate([turns, turns], axis=0) * near_powers)
                near[tile, p * IZ + k, 0], near[tile, p * IZ + k, 1] = c, s
                c, s = turn_pair(turns * far_powers)
                far[tile, p * IZ + k, 0], far[tile, p * IZ + k, 1] = c, s

    def quarters(signs):
        return jnp.concatenate(
            [
                (raw_ref if sign > 0 else negative)[:, q * QUARTER : (q + 1) * QUARTER]
                for q, sign in enumerate(signs)
            ],
            axis=1,
        )

    def keep(values, offsets, part):
        for index, offset in enumerate(offsets):
            group, row = group_of(offset)
            for p in range(POS_HERE):
                spectra[p, group, row : row + CENTRES, part * NE : (part + 1) * NE] = values[
                    index * CENTRES : (index + 1) * CENTRES, p * NE : (p + 1) * NE
                ]

    def filtered(start, p):
        groups = range(start, start + HALF)
        fields = spectra[p, start : start + HALF].reshape(HALF * 2 * CENTRES, 2 * NE)
        fields = jnp.dot(fields, element_ref[...], preferred_element_type=jnp.float32)
        fields = fields.astype(jnp.bfloat16)
        for group in groups:
            scales = [counts[:, 9 + o : 10 + o] for o in PAIRS[group]]
            for block in range(0, CENTRES, 16):
                parts = []
                for half in range(2):
                    row = half * CENTRES + block
                    at = slice(row, row + 16)
                    field = fields[(group - start) * 2 * CENTRES + row :][:16].astype(jnp.float32)
                    scale = scales[half][block : block + 16]
                    re, im = field[:, :NE] * scale, field[:, NE:] * scale
                    cosine, sine = depth_ref[0, group, at, :], depth_ref[1, group, at, :]
                    parts.append([re * cosine - im * sine, re * sine + im * cosine])
                for k in range(IZ):
                    if k > 0:
                        for half in range(2):
                            at = slice(half * CENTRES + block, half * CENTRES + block + 16)
                            cosine, sine = depth_ref[2, group, at, :], depth_ref[3, group, at, :]
                            re, im = parts[half]
                            parts[half] = [re * cosine - im * sine, re * sine + im * cosine]
                    (re, im), (re_low, im_low) = parts
                    if group < GROUPS - 1:
                        values = (re + re_low, im + im_low, re - re_low, im - im_low)
                    else:
                        values = (re, im, re_low, im_low)
                    re, im, re_low, im_low = [value.astype(jnp.bfloat16) for value in values]
                    top = slice(block, block + 16)
                    low = slice(CENTRES + block, CENTRES + block + 16)
                    rows[p * IZ + k, group, top, :NE] = re
                    rows[p * IZ + k, group, top, NE:] = im
                    rows[p * IZ + k, group, low, :NE] = re_low
                    rows[p * IZ + k, group, low, NE:] = im_low

    half_rows = 5 * CENTRES
    left, right = slice(0, QUARTER), slice(QUARTER, 2 * QUARTER)

    def even_bins(index):
        table = even_ref[index]
        signs = (1, 1 - 2 * index, 1, 1 - 2 * index)
        out = transposed_dot(jnp.concatenate([table] * 4, axis=1), quarters(signs)).astype(jnp.bfloat16)
        keep(out[:half_rows], EVEN[index], 0)
        keep(out[half_rows:], EVEN[index], 1)

    def odd_bins(index):
        one, two = odd_ref[:, (left, right)[index]], odd_ref[:, (right, left)[index]]
        signs = ((1, 1, -1, -1), (1, -1, -1, 1))[index]
        out = transposed_dot(
            jnp.concatenate([one, two, one, two], axis=1), quarters(signs)
        ).astype(jnp.bfloat16)
        keep(out[:half_rows], ODD[0], index)
        keep(out[half_rows:], ODD[1], 1 - index)

    for copy in raw_loads + even_loads[0] + even_loads[1]:
        copy.wait()
    for copy in odd_loads + filter_loads + column_loads:
        copy.start()
    even_bins(0)
    for q in range(1, 4):
        negative[:, q * QUARTER : (q + 1) * QUARTER] = -raw_ref[:, q * QUARTER : (q + 1) * QUARTER]
    even_bins(1)
    for copy in odd_loads + filter_loads + column_loads:
        copy.wait()
    filtered(0, 0)
    odd_bins(0)
    filtered(0, 1)
    odd_bins(1)
    filtered(HALF, 0)
    filtered(HALF, 1)

    @pl.loop(0, TILES, unroll=TILES)
    def _(tile):
        weights = column_ref[tile]
        for pk in range(POS_HERE * IZ):
            total_re = jnp.zeros((CENTRES, 128), jnp.float32)
            total_im = jnp.zeros((CENTRES, 128), jnp.float32)
            several = rows[pk].reshape(GROUPS * 2 * CENTRES, 2 * NE)
            several = jnp.dot(several, weights, preferred_element_type=jnp.float32)
            for group, (offset, other) in enumerate(PAIRS):
                first = group * 2 * CENTRES
                both = several[first : first + 2 * CENTRES]
                power = max(offset, other)
                c, s = near[tile, pk, 0, power - 1 : power, :], near[tile, pk, 1, power - 1 : power, :]
                low_re, low_im = both[CENTRES:, :128], both[CENTRES:, 128:]
                if group < GROUPS - 1:
                    total_re += c * both[:CENTRES, :128] - s * low_im
                    total_im += c * both[:CENTRES, 128:] + s * low_re
                else:
                    total_re += both[:CENTRES, :128] + (c * low_re - s * low_im)
                    total_im += both[:CENTRES, 128:] + (c * low_im + s * low_re)
            jump_cos = jnp.broadcast_to(near[tile, pk, 0, 10:11, :], (8, 128))
            jump_sin = jnp.broadcast_to(near[tile, pk, 1, 10:11, :], (8, 128))
            re, im = total_re[CENTRES - 8 :], total_im[CENTRES - 8 :]
            for g in range(CENTRES // 8 - 2, -1, -1):
                re, im = (
                    re * jump_cos - im * jump_sin + total_re[8 * g : 8 * g + 8],
                    re * jump_sin + im * jump_cos + total_im[8 * g : 8 * g + 8],
                )
            value = re * far[tile, pk, 0] - im * far[tile, pk, 1]
            image[tile, pk : pk + 1, :] = jnp.sum(value, axis=0, keepdims=True)

    both = jnp.concatenate([image[tile] for tile in range(TILES)], axis=1)
    is_first = lax.broadcasted_iota(jnp.int32, (POS_HERE * IZ, IX), 0) < IZ
    turn = jnp.where(is_first, probe_ref[0] + probe_anchor, probe_ref[1] + probe_anchor)
    for bit in range(0, 8, 2):
        two = (turn >> bit) & 3
        once, twice, thrice = [pltpu.roll(both, (4 * i << bit) % IX, 1) for i in (1, 2, 3)]
        both = jnp.where(two == 0, both, jnp.where(two == 1, once, jnp.where(two == 2, twice, thrice)))
    scale = 1.0 / math.sqrt(float(NT * NE**3 * NF * 4))
    for tile in range(TILES):
        columns = slice(tile * 128, (tile + 1) * 128)
        partial[tile] = (both[:IZ, columns] + both[IZ:, columns]) * scale

    pl.semaphore_wait(barrier, len(PLANE) + len(PENCIL))
    for index, step in enumerate(PLANE):
        copy = pltpu.make_async_remote_copy(
            src_ref=partial.at[(y + step[0]) & 3],
            dst_ref=inbox.at[index],
            send_sem=send,
            recv_sem=recv,
            device_id=plane_device(*step),
            device_id_type=MESH,
        )
        copy.start()
    pltpu.make_async_copy(inbox, inbox, recv).wait()
    total = partial[y] + jnp.sum(inbox[...], axis=0)
    middle[...] = total
    for index, step in enumerate(PENCIL):
        copy = pltpu.make_async_remote_copy(
            src_ref=middle,
            dst_ref=inbox2.at[index],
            send_sem=send2,
            recv_sem=recv2,
            device_id=pencil_device(*step),
            device_id_type=MESH,
        )
        copy.start()
    pltpu.make_async_copy(inbox2, inbox2, recv2).wait()
    total = total + jnp.sum(inbox2[...], axis=0)
    out_ref[...] = pltpu.roll(total, (128 - (x_chip * 32 + z_chip * 4)) & 127, 1)
    pltpu.make_async_copy(inbox, inbox, send).wait()
    pltpu.make_async_copy(inbox2, inbox2, send2).wait()


def focus(raw, band_bins, probe_index):
    even, odd = time_tables()
    tables = [even, odd, element_table(), column_table(), depth_table()]
    vmem = pl.BlockSpec(memory_space=pltpu.VMEM)
    smem = pl.BlockSpec(memory_space=pltpu.SMEM)
    hbm = pl.BlockSpec(memory_space=pltpu.HBM)
    held = [pltpu.VMEM((POS_HERE * NE, NT), jnp.bfloat16)]
    held += [pltpu.VMEM(table.shape, table.dtype) for table in tables]
    tile = (IZ, 128)
    return pl.pallas_call(
        focus_kernel,
        out_shape=jax.ShapeDtypeStruct(tile, jnp.float32),
        in_specs=[smem, vmem] + [hbm] * 6,
        out_specs=vmem,
        scratch_shapes=[
            *held,
            pltpu.SemaphoreType.DMA((16,)),
            pltpu.VMEM((POS_HERE * NE, NT), jnp.bfloat16),
            pltpu.VMEM((POS_HERE, GROUPS, 2 * CENTRES, 2 * NE), jnp.bfloat16),
            pltpu.VMEM((POS_HERE * IZ, GROUPS, 2 * CENTRES, 2 * NE), jnp.bfloat16),
            pltpu.VMEM((CENTRES, 32), jnp.float32),
            pltpu.VMEM((TILES, POS_HERE * IZ, 2, 16, 128), jnp.float32),
            pltpu.VMEM((TILES, POS_HERE * IZ, 2, 8, 128), jnp.float32),
            pltpu.VMEM((TILES, POS_HERE * IZ, 128), jnp.float32),
            pltpu.VMEM((TILES, *tile), jnp.float32),
            pltpu.VMEM((15, *tile), jnp.float32),
            pltpu.VMEM(tile, jnp.float32),
            pltpu.VMEM((15, *tile), jnp.float32),
            pltpu.SemaphoreType.DMA,
            pltpu.SemaphoreType.DMA,
            pltpu.SemaphoreType.DMA,
            pltpu.SemaphoreType.DMA,
        ],
        compiler_params=pltpu.CompilerParams(
            collective_id=0, has_side_effects=True, vmem_limit_bytes=63 * 1024 * 1024
        ),
        name="focus",
    )(
        probe_index,
        band_bins.reshape(1, NF),
        raw.reshape(POS_HERE * NE, NT),
        *[jnp.asarray(table) for table in tables],
    )


def per_device(raw_capture, band_bins, probe_index):
    return focus(raw_capture, band_bins, probe_index)[:, :4]


def solution(mesh):
    in_specs = (P("pos", ("section", "freq"), None, None), P(), P("pos"))
    out_specs = P(None, ("section", "freq"))
    return jax.shard_map(
        per_device, mesh=mesh, in_specs=in_specs, out_specs=out_specs, check_vma=False
    )
```

```python
import math

import jax
import jax.numpy as jnp
import ml_dtypes
import numpy as np
from jax import lax
from jax.experimental import pallas as pl
from jax.experimental.pallas import tpu as pltpu
from jax.sharding import PartitionSpec as P

NE = 128
NT = 4096
NF = 1024
IX = 512
IZ = 4
POS_HERE = 2
QUARTER = NT // 4
LOWEST = 64
CENTRES = 48
SPACING = 20
FIRST = LOWEST + 9
PAIRS = ((1, -1), (3, -3), (5, -5), (7, -7), (9, -9), (2, -2), (4, -4), (6, -6), (8, -8), (0, 10))
GROUPS = len(PAIRS)
HALF = GROUPS // 2
TILES = IX // 128
MESH = pl.DeviceIdType.MESH

wave_speed = 0.5
pixel_pitch = 0.25
depth_start = 20.0
probe_anchor = 32

EVEN = ((-9, -5, -1, 3, 7), (-7, -3, 1, 5, 9))
ODD = ((-8, -4, 0, 4, 8), (-6, -2, 2, 6, 10))


def group_of(offset):
    group = [offset in pair for pair in PAIRS].index(True)
    return group, CENTRES * PAIRS[group].index(offset)


def time_tables():
    samples = np.arange(QUARTER)
    centres = FIRST + SPACING * np.arange(CENTRES)

    def parts(offsets):
        bins = np.concatenate([centres + offset for offset in offsets])
        angle = 2.0 * np.pi * (bins[:, None] * samples[None, :] % NT) / NT
        return np.cos(angle), -np.sin(angle)

    even = np.stack([np.concatenate(parts(offsets), axis=0) for offsets in EVEN])
    re1, im1 = parts(ODD[0])
    re3, im3 = parts(ODD[1])
    odd = np.concatenate(
        [np.concatenate([re1, im1], axis=1), np.concatenate([im3, re3], axis=1)], axis=0
    )
    return even.astype(ml_dtypes.bfloat16), odd.astype(ml_dtypes.bfloat16)


def element_table():
    pos = np.arange(NE) - (NE - 1) / 2.0
    angle = pos[:, None] * (np.arange(NE) - NE // 2)[None, :] * (2.0 * np.pi / NE)
    c, s = np.cos(angle), np.sin(angle)
    table = np.concatenate([np.concatenate([c, -s], axis=1), np.concatenate([s, c], axis=1)], axis=0)
    return table.astype(ml_dtypes.bfloat16)


def column_table():
    order = np.arange(NE) - NE // 2
    angle = 2.0 * np.pi * (order[:, None] * np.arange(IX)[None, :] % IX) / IX
    cosine, sine = np.cos(angle), np.sin(angle)
    tiles = []
    for start in range(0, IX, 128):
        c, s = cosine[:, start : start + 128], sine[:, start : start + 128]
        tiles.append(
            np.concatenate([np.concatenate([c, s], axis=1), np.concatenate([-s, c], axis=1)], axis=0)
        )
    return np.stack(tiles).astype(ml_dtypes.bfloat16)


def depth_table():
    centres = FIRST + SPACING * np.arange(CENTRES)
    wavenumber = (np.arange(NE) - NE // 2) * (2.0 * np.pi / NE)

    def parts(offset):
        k = (centres + offset)[:, None] * (2.0 * np.pi / NT) / wave_speed
        vertical = np.sqrt(np.maximum(k * k - wavenumber[None, :] ** 2, 0.0))
        weight = vertical / k
        first = weight * np.exp(1j * vertical * depth_start)
        step = np.exp(1j * vertical * pixel_pitch)
        return np.stack([first.real, first.imag, step.real, step.imag])

    groups = [
        np.concatenate([parts(offset) for offset in pair], axis=1) for pair in PAIRS
    ]
    return np.stack(groups, axis=1).astype(np.float32)


def turn_pair(turns):
    x = turns - jnp.floor(turns + 0.5)
    square = x * x
    sine = jnp.full_like(x, math.pi**13 / math.factorial(13))
    for power in (11, 9, 7, 5, 3, 1):
        sign = 1.0 if power % 4 == 1 else -1.0
        sine = sine * square + sign * math.pi**power / math.factorial(power)
    sine = sine * x
    cosine = jnp.full_like(x, math.pi**12 / math.factorial(12))
    for power in (10, 8, 6, 4, 2, 0):
        sign = 1.0 if power % 4 == 0 else -1.0
        cosine = cosine * square + sign * math.pi**power / math.factorial(power)
    return 1.0 - 2.0 * sine * sine, 2.0 * sine * cosine


def transposed_dot(a, b):
    return lax.dot_general(a, b, (((1,), (1,)), ((), ())), preferred_element_type=jnp.float32)


def hops(count, delta):
    return min(delta, count - delta)


PLANE = sorted(
    [(dy, dx) for dy in range(4) for dx in range(4) if dy or dx],
    key=lambda d: -(hops(4, d[0]) + hops(4, d[1])),
)
PENCIL = sorted(
    [(dz, dc) for dz in range(8) for dc in range(2) if dz or dc],
    key=lambda d: -(2 * hops(8, d[0]) + d[1]),
)


def focus_kernel(
    probe_ref, bins_ref, raw_hbm, even_hbm, odd_hbm, element_hbm, column_hbm, depth_hbm,
    out_ref,
    raw_ref, even_ref, odd_ref, element_ref, column_ref, depth_ref, loaded,
    negative, spectra, rows, counts, near, far, image,
    partial, inbox, middle, inbox2, send, recv, send2, recv2,
):
    section, freq, core = lax.axis_index("section"), lax.axis_index("freq"), lax.axis_index("pos")
    y, x_chip, z_chip = section * 2 + (freq >> 5), (freq >> 3) & 3, freq & 7

    def plane_device(dy, dx):
        yy, xx = (y + dy) & 3, (x_chip + dx) & 3
        return (yy >> 1, (yy & 1) * 32 + xx * 8 + z_chip, core)

    def pencil_device(dz, dc):
        return (section, (freq & 56) + ((z_chip + dz) & 7), (core + dc) & 1)

    def pieces(first, source, target, count):
        step = source.shape[0] // count
        return [
            pltpu.make_async_copy(
                source.at[pl.ds(i * step, step)], target.at[pl.ds(i * step, step)], loaded.at[first + i]
            )
            for i in range(count)
        ]

    raw_loads = pieces(0, raw_hbm, raw_ref, 4)
    even_loads = [pieces(4 + 2 * i, even_hbm.at[i], even_ref.at[i], 2) for i in range(2)]
    odd_loads = pieces(8, odd_hbm, odd_ref, 2)
    filter_loads = pieces(10, element_hbm, element_ref, 1) + pieces(11, depth_hbm, depth_ref, 4)
    column_loads = pieces(15, column_hbm, column_ref, 1)
    for copy in raw_loads + even_loads[0] + even_loads[1]:
        copy.start()

    bins = bins_ref[...] - LOWEST
    centre = (bins * 3277) >> 16
    offset = bins - SPACING * centre
    is_centre = jnp.where(lax.broadcasted_iota(jnp.int32, (CENTRES, NF), 0) == centre, 1.0, 0.0)
    is_offset = jnp.where(lax.broadcasted_iota(jnp.int32, (32, NF), 0) == offset, 1.0, 0.0)
    counts[...] = transposed_dot(is_centre.astype(jnp.bfloat16), is_offset.astype(jnp.bfloat16))

    tx_coord = (section * 64 + freq).astype(jnp.float32) - (NE - 1) / 2.0
    sub = lax.broadcasted_iota(jnp.int32, (16, 128), 0).astype(jnp.float32)
    near_powers = jnp.where(sub < 10.0, sub + 1.0, SPACING * 8.0)
    far_powers = FIRST + SPACING * sub[:8]
    lane = lax.broadcasted_iota(jnp.int32, (8, 128), 1)
    for p in range(POS_HERE):
        shift = 4 * (probe_ref[p] + probe_anchor)
        centre_here = (probe_ref[p] + probe_anchor).astype(jnp.float32)
        for tile in range(TILES):
            column = ((lane + (128 * tile + shift)) & (IX - 1)).astype(jnp.float32)
            x = (pixel_pitch * column - centre_here) - tx_coord
            for k in range(IZ):
                z = depth_start + pixel_pitch * k
                turns = jnp.sqrt(x * x + z * z) * (1.0 / (NT * wave_speed))
                c, s = turn_pair(jnp.concatenate([turns, turns], axis=0) * near_powers)
                near[tile, p * IZ + k, 0], near[tile, p * IZ + k, 1] = c, s
                c, s = turn_pair(turns * far_powers)
                far[tile, p * IZ + k, 0], far[tile, p * IZ + k, 1] = c, s

    def quarters(signs):
        return jnp.concatenate(
            [
                (raw_ref if sign > 0 else negative)[:, q * QUARTER : (q + 1) * QUARTER]
                for q, sign in enumerate(signs)
            ],
            axis=1,
        )

    def keep(values, offsets, part):
        for index, offset in enumerate(offsets):
            group, row = group_of(offset)
            for p in range(POS_HERE):
                spectra[p, group, row : row + CENTRES, part * NE : (part + 1) * NE] = values[
                    index * CENTRES : (index + 1) * CENTRES, p * NE : (p + 1) * NE
                ]

    def filtered(start, p):
        groups = range(start, start + HALF)
        fields = spectra[p, start : start + HALF].reshape(HALF * 2 * CENTRES, 2 * NE)
        fields = jnp.dot(fields, element_ref[...], preferred_element_type=jnp.float32)
        fields = fields.astype(jnp.bfloat16)
        for group in groups:
            scales = [counts[:, 9 + o : 10 + o] for o in PAIRS[group]]
            for block in range(0, CENTRES, 16):
                parts = []
                for half in range(2):
                    row = half * CENTRES + block
                    at = slice(row, row + 16)
                    field = fields[(group - start) * 2 * CENTRES + row :][:16].astype(jnp.float32)
                    scale = scales[half][block : block + 16]
                    re, im = field[:, :NE] * scale, field[:, NE:] * scale
                    cosine, sine = depth_ref[0, group, at, :], depth_ref[1, group, at, :]
                    parts.append([re * cosine - im * sine, re * sine + im * cosine])
                for k in range(IZ):
                    if k > 0:
                        for half in range(2):
                            at = slice(half * CENTRES + block, half * CENTRES + block + 16)
                            cosine, sine = depth_ref[2, group, at, :], depth_ref[3, group, at, :]
                            re, im = parts[half]
                            parts[half] = [re * cosine - im * sine, re * sine + im * cosine]
                    (re, im), (re_low, im_low) = parts
                    if group < GROUPS - 1:
                        values = (re + re_low, im + im_low, re - re_low, im - im_low)
                    else:
                        values = (re, im, re_low, im_low)
                    re, im, re_low, im_low = [value.astype(jnp.bfloat16) for value in values]
                    top = slice(block, block + 16)
                    low = slice(CENTRES + block, CENTRES + block + 16)
                    rows[p * IZ + k, group, top, :NE] = re
                    rows[p * IZ + k, group, top, NE:] = im
                    rows[p * IZ + k, group, low, :NE] = re_low
                    rows[p * IZ + k, group, low, NE:] = im_low

    half_rows = 5 * CENTRES
    left, right = slice(0, QUARTER), slice(QUARTER, 2 * QUARTER)

    def even_bins(index):
        table = even_ref[index]
        signs = (1, 1 - 2 * index, 1, 1 - 2 * index)
        out = transposed_dot(jnp.concatenate([table] * 4, axis=1), quarters(signs)).astype(jnp.bfloat16)
        keep(out[:half_rows], EVEN[index], 0)
        keep(out[half_rows:], EVEN[index], 1)

    def odd_bins(index):
        one, two = odd_ref[:, (left, right)[index]], odd_ref[:, (right, left)[index]]
        signs = ((1, 1, -1, -1), (1, -1, -1, 1))[index]
        out = transposed_dot(
            jnp.concatenate([one, two, one, two], axis=1), quarters(signs)
        ).astype(jnp.bfloat16)
        keep(out[:half_rows], ODD[0], index)
        keep(out[half_rows:], ODD[1], 1 - index)

    for copy in raw_loads + even_loads[0] + even_loads[1]:
        copy.wait()
    for copy in odd_loads + filter_loads + column_loads:
        copy.start()
    even_bins(0)
    for q in range(1, 4):
        negative[:, q * QUARTER : (q + 1) * QUARTER] = -raw_ref[:, q * QUARTER : (q + 1) * QUARTER]
    even_bins(1)
    barrier = pltpu.get_barrier_semaphore()
    for step in PLANE:
        pl.semaphore_signal(barrier, inc=1, device_id=plane_device(*step), device_id_type=MESH)
    for step in PENCIL:
        pl.semaphore_signal(barrier, inc=1, device_id=pencil_device(*step), device_id_type=MESH)
    for copy in odd_loads + filter_loads + column_loads:
        copy.wait()
    filtered(0, 0)
    odd_bins(0)
    filtered(0, 1)
    odd_bins(1)
    filtered(HALF, 0)
    filtered(HALF, 1)

    @pl.loop(0, TILES, unroll=TILES)
    def _(tile):
        weights = column_ref[tile]
        for pk in range(POS_HERE * IZ):
            total_re = jnp.zeros((CENTRES, 128), jnp.float32)
            total_im = jnp.zeros((CENTRES, 128), jnp.float32)
            several = rows[pk].reshape(GROUPS * 2 * CENTRES, 2 * NE)
            several = jnp.dot(several, weights, preferred_element_type=jnp.float32)
            for group, (offset, other) in enumerate(PAIRS):
                first = group * 2 * CENTRES
                both = several[first : first + 2 * CENTRES]
                power = max(offset, other)
                c, s = near[tile, pk, 0, power - 1 : power, :], near[tile, pk, 1, power - 1 : power, :]
                low_re, low_im = both[CENTRES:, :128], both[CENTRES:, 128:]
                if group < GROUPS - 1:
                    total_re += c * both[:CENTRES, :128] - s * low_im
                    total_im += c * both[:CENTRES, 128:] + s * low_re
                else:
                    total_re += both[:CENTRES, :128] + (c * low_re - s * low_im)
                    total_im += both[:CENTRES, 128:] + (c * low_im + s * low_re)
            jump_cos = jnp.broadcast_to(near[tile, pk, 0, 10:11, :], (8, 128))
            jump_sin = jnp.broadcast_to(near[tile, pk, 1, 10:11, :], (8, 128))
            re, im = total_re[CENTRES - 8 :], total_im[CENTRES - 8 :]
            for g in range(CENTRES // 8 - 2, -1, -1):
                re, im = (
                    re * jump_cos - im * jump_sin + total_re[8 * g : 8 * g + 8],
                    re * jump_sin + im * jump_cos + total_im[8 * g : 8 * g + 8],
                )
            value = re * far[tile, pk, 0] - im * far[tile, pk, 1]
            image[tile, pk : pk + 1, :] = jnp.sum(value, axis=0, keepdims=True)

    both = jnp.concatenate([image[tile] for tile in range(TILES)], axis=1)
    is_first = lax.broadcasted_iota(jnp.int32, (POS_HERE * IZ, IX), 0) < IZ
    turn = jnp.where(is_first, probe_ref[0] + probe_anchor, probe_ref[1] + probe_anchor)
    for bit in range(0, 8, 2):
        two = (turn >> bit) & 3
        once, twice, thrice = [pltpu.roll(both, (4 * i << bit) % IX, 1) for i in (1, 2, 3)]
        both = jnp.where(two == 0, both, jnp.where(two == 1, once, jnp.where(two == 2, twice, thrice)))
    scale = 1.0 / math.sqrt(float(NT * NE**3 * NF * 4))
    for tile in range(TILES):
        columns = slice(tile * 128, (tile + 1) * 128)
        partial[tile] = (both[:IZ, columns] + both[IZ:, columns]) * scale

    pl.semaphore_wait(barrier, len(PLANE) + len(PENCIL))
    for index, step in enumerate(PLANE):
        copy = pltpu.make_async_remote_copy(
            src_ref=partial.at[(y + step[0]) & 3],
            dst_ref=inbox.at[index],
            send_sem=send,
            recv_sem=recv,
            device_id=plane_device(*step),
            device_id_type=MESH,
        )
        copy.start()
    pltpu.make_async_copy(inbox, inbox, recv).wait()
    total = partial[y] + jnp.sum(inbox[...], axis=0)
    middle[...] = total
    for index, step in enumerate(PENCIL):
        copy = pltpu.make_async_remote_copy(
            src_ref=middle,
            dst_ref=inbox2.at[index],
            send_sem=send2,
            recv_sem=recv2,
            device_id=pencil_device(*step),
            device_id_type=MESH,
        )
        copy.start()
    pltpu.make_async_copy(inbox2, inbox2, recv2).wait()
    total = total + jnp.sum(inbox2[...], axis=0)
    out_ref[...] = pltpu.roll(total, (128 - (x_chip * 32 + z_chip * 4)) & 127, 1)
    pltpu.make_async_copy(inbox, inbox, send).wait()
    pltpu.make_async_copy(inbox2, inbox2, send2).wait()


def focus(raw, band_bins, probe_index):
    even, odd = time_tables()
    tables = [even, odd, element_table(), column_table(), depth_table()]
    vmem = pl.BlockSpec(memory_space=pltpu.VMEM)
    smem = pl.BlockSpec(memory_space=pltpu.SMEM)
    hbm = pl.BlockSpec(memory_space=pltpu.HBM)
    held = [pltpu.VMEM((POS_HERE * NE, NT), jnp.bfloat16)]
    held += [pltpu.VMEM(table.shape, table.dtype) for table in tables]
    tile = (IZ, 128)
    return pl.pallas_call(
        focus_kernel,
        out_shape=jax.ShapeDtypeStruct(tile, jnp.float32),
        in_specs=[smem, vmem] + [hbm] * 6,
        out_specs=vmem,
        scratch_shapes=[
            *held,
            pltpu.SemaphoreType.DMA((16,)),
            pltpu.VMEM((POS_HERE * NE, NT), jnp.bfloat16),
            pltpu.VMEM((POS_HERE, GROUPS, 2 * CENTRES, 2 * NE), jnp.bfloat16),
            pltpu.VMEM((POS_HERE * IZ, GROUPS, 2 * CENTRES, 2 * NE), jnp.bfloat16),
            pltpu.VMEM((CENTRES, 32), jnp.float32),
            pltpu.VMEM((TILES, POS_HERE * IZ, 2, 16, 128), jnp.float32),
            pltpu.VMEM((TILES, POS_HERE * IZ, 2, 8, 128), jnp.float32),
            pltpu.VMEM((TILES, POS_HERE * IZ, 128), jnp.float32),
            pltpu.VMEM((TILES, *tile), jnp.float32),
            pltpu.VMEM((15, *tile), jnp.float32),
            pltpu.VMEM(tile, jnp.float32),
            pltpu.VMEM((15, *tile), jnp.float32),
            pltpu.SemaphoreType.DMA,
            pltpu.SemaphoreType.DMA,
            pltpu.SemaphoreType.DMA,
            pltpu.SemaphoreType.DMA,
        ],
        compiler_params=pltpu.CompilerParams(
            collective_id=0, has_side_effects=True, vmem_limit_bytes=63 * 1024 * 1024
        ),
        name="focus",
    )(
        probe_index,
        band_bins.reshape(1, NF),
        raw.reshape(POS_HERE * NE, NT),
        *[jnp.asarray(table) for table in tables],
    )


def per_device(raw_capture, band_bins, probe_index):
    return focus(raw_capture, band_bins, probe_index)[:, :4]


def solution(mesh):
    in_specs = (P("pos", ("section", "freq"), None, None), P(), P("pos"))
    out_specs = P(None, ("section", "freq"))
    return jax.shard_map(
        per_device, mesh=mesh, in_specs=in_specs, out_specs=out_specs, check_vma=False
    )
```
